512 devices in a mesh: member: 16 (over z, core), tile: 32 (over y, x).
Axes of the slice: x: 4, y: 8, z: 8, core: 2. Of those that a mesh axis runs over, the one named last changes fastest.
Arguments:
- control: float32 [16, 96, 8, 4096], P('member', None, None, 'tile'), may hold values from -70 to 70
- members: bfloat16 [16, 96, 8, 4096], P('member', None, None, 'tile'), may hold values from -4 to 4
- obs_weight: float32 [96, 8, 4096], P(None, None, 'tile'), may hold values from 0.3 to 3
- innovation: float32 [96, 8, 4096], P(None, None, 'tile'), may hold values from -5 to 5
- scale_index: int32 [96], replicated, may hold values from 0 to 3
Outputs:
- increment: float32 [96, 8, 4096], P('member', None, 'tile')
- gradient: float32 [16, 96, 8, 4096], P('member', None, None, 'tile')
- cost_value: float32 [], replicated
- mean_square: float32 [], replicated
The draws below stay inside these ranges and needn't reach their ends.
All inputs are finite; a program needn't handle non-finite values.
Results may differ from the reference program's by a relative error of at most 0.0003.
Values sent between devices are 32-bit elements; how exact they have to be, the bound alone decides.
No kernel may reach another device: no remote copies, remote signals or barrier semaphores. Data moves between devices by JAX's collectives and lax.ppermute only.
A program may use at most 64 MiB of HBM per device.

```python
import math
import jax
import jax.numpy as jnp
from jax import lax

LEV = 96
LAT = 8
HALF = 64
NLON = 4096
MEMBERS = 16


def draw_control(key, part):
    key = jax.random.fold_in(key, 7)
    subkeys = jax.random.split(key, 2)
    member_ramp = jnp.arange(MEMBERS).astype(jnp.float32) / (MEMBERS - 1)
    member_scale = jnp.exp(jnp.log(3.0) * member_ramp)[:, None, None, None]
    column_scale = 0.3 * jnp.exp(jnp.log(10.0) * jax.random.uniform(subkeys[1], (1, 1, LAT, NLON)))
    base_draw = jnp.clip(jax.random.normal(subkeys[0], (MEMBERS, LEV, LAT, NLON)), -4.0, 4.0)
    return base_draw * member_scale * column_scale


def place_ends(values, rng, smallest, top_value):
    longest = values.shape.index(max(values.shape))
    spots = []
    for shift in (0, 1):
        where = [jax.random.randint(jax.random.fold_in(rng, axis), (), 0, length) for axis, length in enumerate(values.shape)]
        where[longest] = (where[longest] + shift) % values.shape[longest]
        spots.append(tuple(where))
    return values.at[spots[0]].set(smallest).at[spots[1]].set(top_value)


def block_levels(own_key, dims, shards, smallest, largest):
    def one(dim, blocks):
        draws = jax.random.uniform(jax.random.fold_in(jax.random.fold_in(own_key, 6), dim), (blocks,), jnp.float32, smallest / len(shards), largest / len(shards))
        return jnp.repeat(jnp.exp(draws), dims[dim] // blocks).reshape((-1,) + (1,) * (len(dims) - dim - 1))

    level = one(*shards[0])
    for cut in shards[1:]:
        level = level * one(*cut)
    return level


def normal_values(stream_key, extent, scale, bound, cuts=(), kind=jnp.bfloat16):
    values = jax.random.normal(stream_key, extent, jnp.float32) * scale
    if len(cuts) > 0:
        values = block_levels(stream_key, extent, cuts, -0.22, 0.18) * values
    return jnp.clip(values, min=-bound, max=bound).astype(kind)


def setup_inputs(seed: int = 0) -> dict:
    keys = jax.random.split(jax.random.key(seed), 6)
    control = draw_control(jax.random.fold_in(keys[5], 71), 0)
    members = normal_values(keys[1], (MEMBERS, LEV, LAT, NLON), 1.0, 4.0, ((0, 16), (3, 32)))
    obs_weight = jnp.clip(jnp.exp(math.log(3.0) - 2.3025851 * jax.random.uniform(keys[2], (LEV, LAT, NLON), jnp.float32) ** block_levels(keys[2], (LEV, LAT, NLON), ((2, 32),), -0.2, 0.2)), 0.3, 3.0)
    innovation = normal_values(keys[3], (LEV, LAT, NLON), 1.0, 5.0, ((2, 32),), jnp.float32)
    scale_index = place_ends(jax.random.randint(keys[4], (LEV,), 0, 4), jax.random.fold_in(keys[4], 1), 0, 3).astype(jnp.int32)
    return {"control": control, "members": members, "obs_weight": obs_weight, "innovation": innovation, "scale_index": scale_index}


precise = lax.Precision.HIGHEST

def vertical_matrix(level_scale):
    levels = jnp.arange(level_scale.shape[0]).astype(jnp.float32)
    spacing = levels[:, None] - levels[None, :]
    spread = level_scale[:, None] * level_scale[:, None] + level_scale[None, :] * level_scale[None, :]
    return jnp.exp(-spacing * spacing / spread)

def lon_bands(level_scale, half_width):
    spread_lon = half_width * level_scale / 4.0
    inputs = jnp.arange(3 * half_width).astype(jnp.float32)[:, None]
    outputs = jnp.arange(half_width).astype(jnp.float32)[None, :]
    spacing = inputs - half_width - outputs
    distance = jnp.arange(-half_width, half_width + 1).astype(jnp.float32)
    squared = spread_lon[:, None] * spread_lon[:, None]
    norm_sum = jnp.sqrt(lax.optimization_barrier(jnp.sum(jnp.exp(-distance[None, :] * distance[None, :] / squared), axis=1)))
    weight = jnp.exp(-spacing[None] * spacing[None] / (2.0 * spread_lon[:, None, None] * spread_lon[:, None, None]))
    weight = jnp.where(jnp.abs(spacing)[None] <= half_width, weight, 0.0)
    return weight / norm_sum[:, None, None]

def lat_matrix(level_scale, lat_rows):
    spread_lat = lat_rows * level_scale / 8.0
    positions = jnp.arange(lat_rows).astype(jnp.float32)
    spacing = positions[:, None] - positions[None, :]
    distance = jnp.arange(-(lat_rows - 1), lat_rows).astype(jnp.float32)
    squared = spread_lat[:, None] * spread_lat[:, None]
    norm_sum = jnp.sqrt(lax.optimization_barrier(jnp.sum(jnp.exp(-distance[None, :] * distance[None, :] / squared), axis=1)))
    weight = jnp.exp(-spacing[None] * spacing[None] / (2.0 * spread_lat[:, None, None] * spread_lat[:, None, None]))
    return weight / norm_sum[:, None, None]

def apply_lon(blocks, banded):
    windows = jnp.concatenate([blocks[:, :, :-2], blocks[:, :, 1:-1], blocks[:, :, 2:]], axis=3)
    result = jnp.einsum('lakd,ldj->lakj', windows, banded, precision=precise)
    return result.reshape(result.shape[0], result.shape[1], -1)

def vertical_apply(matrix, values):
    return jnp.einsum('kq,qao->kao', matrix, values, precision=precise)

def lat_apply(matrix, values):
    return jnp.einsum('lab,lbo->lao', matrix, values, precision=precise)

def lon_periodic(values, banded, half_width):
    blocks = values.reshape(values.shape[0], values.shape[1], -1, half_width)
    blocks = jnp.concatenate([blocks[:, :, -1:], blocks, blocks[:, :, :1]], axis=2)
    return apply_lon(blocks, banded)

def reference(control, members, obs_weight, innovation, scale_index):
    level_scale = 1.0 + scale_index.astype(jnp.float32)
    vertical = vertical_matrix(level_scale)
    banded = lon_bands(level_scale, HALF)
    meridional = lat_matrix(level_scale, LAT)
    inverse = 1.0 / jnp.sqrt(jnp.float32(MEMBERS - 1))
    cell_count = float(MEMBERS * LEV * LAT * NLON)

    def forward_member(couple):
        control_one, member_one = couple
        alpha_field = lat_apply(meridional, lon_periodic(vertical_apply(vertical, control_one), banded, HALF))
        return member_one.astype(jnp.float32) * alpha_field * inverse
    member_terms = lax.map(forward_member, (control, members))
    increment = lax.optimization_barrier(jnp.sum(member_terms, axis=0))
    misfit = obs_weight * increment - innovation

    def adjoint_member(couple):
        control_one, member_one = couple
        weighted = member_one.astype(jnp.float32) * misfit * inverse
        adjoint_field = vertical_apply(vertical, lon_periodic(lat_apply(meridional, weighted), banded, HALF))
        return control_one + adjoint_field
    gradient = lax.map(adjoint_member, (control, members))
    cost_value = (0.5 * jnp.sum(control * control) + jnp.sum(0.5 * obs_weight * increment * increment - innovation * increment)) / cell_count
    mean_square = jnp.sum(gradient * gradient) / cell_count
    return (increment, gradient, cost_value, mean_square)
```

```python
import functools

import jax
import jax.numpy as jnp
import numpy as np
from jax import lax
from jax.experimental import pallas as pl
from jax.experimental.pallas import tpu as pltpu
from jax.sharding import PartitionSpec as P

CLASSES = 4
VMEM_LIMIT = 48 * 1024 * 1024
f32, bf16 = jnp.float32, jnp.bfloat16


def vmem(count):
    return [pl.BlockSpec(memory_space=pltpu.VMEM)] * count


def smem():
    return pl.BlockSpec(memory_space=pltpu.SMEM)


def params():
    return pltpu.CompilerParams(vmem_limit_bytes=VMEM_LIMIT)


def split(value):
    high = value.astype(bf16)
    low = (value - high.astype(f32)).astype(bf16)
    return high, low


def dot(a, b):
    return jnp.dot(a, b, preferred_element_type=f32)


def left_product(high, low, value):
    vhigh, vlow = split(value)
    width = value.shape[1]
    both = dot(high, jnp.concatenate([vhigh, vlow], axis=1))
    return both[:, :width] + both[:, width:] + dot(low, vhigh)


def band_product(value, high, low):
    vhigh, vlow = split(value)
    return dot(vhigh, high) + dot(vlow, high) + dot(vhigh, low)


def lane_is_low(shape, half):
    return lax.broadcasted_iota(jnp.int32, shape, len(shape) - 1) < half


def pack_halves(x, to_right, to_left):
    half_levels, _, columns = to_right.shape
    half = columns // 2
    first = x[:half_levels]
    second = x[half_levels:]
    turned = pltpu.roll(second.reshape(-1, columns), half, 1).reshape(second.shape)
    low = lane_is_low(first.shape, half)
    to_right[...] = jnp.where(low, turned, first)
    to_left[...] = jnp.where(low, first, turned)


def unpack_halves(from_left, from_right):
    columns = from_left.shape[2]
    half = columns // 2
    low = lane_is_low(from_left.shape, half)
    first = jnp.where(low, from_right, from_left).reshape(-1, columns)
    second = pltpu.roll(jnp.where(low, from_left, from_right).reshape(-1, columns), half, 1)
    return jnp.concatenate([first, second], axis=0)


def pick_class(classes, all_ref, out_ref, rows, columns):
    for level in range(out_ref.shape[0] // rows):
        at = pl.multiple_of(classes[level] * columns, columns)
        out_ref[pl.ds(level * rows, rows), :] = all_ref[pl.ds(level * rows, rows), pl.ds(at, columns)]


def pack_kernel(x_ref, right_ref, left_ref):
    pack_halves(x_ref[...], right_ref, left_ref)


def class_scale(c):
    return 1.0 + float(c)


def prep_kernel(classes, col_ref, row_ref, x_ref, fh_ref, fl_ref, ah_ref, al_ref, bh_ref, bl_ref, y_ref, sum_ref, wide_ref, pat_ref):
    levels, lat, columns = x_ref.shape
    rows = levels * lat
    half = columns // 2
    scale_col = 1.0 + col_ref[...].astype(f32)
    scale_row = 1.0 + row_ref[...].astype(f32)
    k = lax.broadcasted_iota(jnp.int32, (levels, levels), 0).astype(f32)
    q = lax.broadcasted_iota(jnp.int32, (levels, levels), 1).astype(f32)
    spacing = k - q
    vertical = jnp.exp(-spacing * spacing / (scale_col * scale_col + scale_row * scale_row))
    which = lax.broadcasted_iota(jnp.int32, (levels, rows), 1) // lat
    spread = (which == lax.broadcasted_iota(jnp.int32, (levels, rows), 0)).astype(f32).astype(bf16)
    vh, vl = split(vertical)
    wide_ref[...] = dot(vh, spread) + dot(vl, spread)
    row8 = jnp.broadcast_to(row_ref[...].astype(f32), (8, levels)).astype(bf16)
    class_wide = dot(row8, spread)[:1]
    i = lax.broadcasted_iota(jnp.int32, (lat, rows), 0)
    j = lax.broadcasted_iota(jnp.int32, (lat, rows), 1) % lat
    gap = (i - j).astype(f32)
    own = jnp.zeros((lat, rows), f32)
    for c in range(CLASSES):
        rho = lat * class_scale(c) / 8.0
        e = np.arange(-(lat - 1), lat, dtype=np.float32)
        norm = float(np.sqrt(np.sum(np.exp(-e * e / np.float32(rho * rho)), dtype=np.float32)))
        pattern = jnp.exp(-gap * gap / (2.0 * rho * rho)) / norm
        pat_ref[c] = pattern
        own = jnp.where(class_wide == float(c), pattern, own)
    for pair in range(levels // 2):
        forward, adjoint = [], []
        for level in (2 * pair, 2 * pair + 1):
            line = wide_ref[pl.ds(level, 1), :]
            forward.append(line * pat_ref[classes[level]])
            adjoint.append(line * own)
        at = pl.ds(2 * pair * lat, 2 * lat)
        fh_ref[at, :], fl_ref[at, :] = split(jnp.concatenate(forward, axis=0))
        ah_ref[at, :], al_ref[at, :] = split(jnp.concatenate(adjoint, axis=0))
    d = lax.broadcasted_iota(jnp.int32, (2 * columns, columns), 0)
    out = lax.broadcasted_iota(jnp.int32, (2 * columns, columns), 1)
    place = jnp.where(d < columns, d, jnp.where(d < columns + half, d, d - 2 * columns))
    far = (place - out).astype(f32)
    inside = jnp.abs(far) <= half
    for c in range(CLASSES):
        sigma = half * class_scale(c) / 4.0
        e = np.arange(-half, half + 1, dtype=np.float32)
        norm = float(np.sqrt(np.sum(np.exp(-e * e / np.float32(sigma * sigma)), dtype=np.float32)))
        band = jnp.where(inside, jnp.exp(-far * far / (2.0 * sigma * sigma)) / norm, 0.0)
        at = pl.ds(c * columns, columns)
        bh_ref[:, at], bl_ref[:, at] = split(band)
    x = x_ref[...].reshape(rows, columns)
    sum_ref[...] = 0.5 * jnp.sum(x * x, axis=0, keepdims=True)
    y_ref[...] = left_product(fh_ref[...], fl_ref[...], x)


def forward_kernel(inverse, classes, fl_in, fr_in, y_ref, fh_ref, flo_ref, bh_ref, bl_ref, m_ref, out_ref, all_ref, picked_ref):
    levels, lat, columns = m_ref.shape
    halo = left_product(fh_ref[...], flo_ref[...], unpack_halves(fl_in[...], fr_in[...]))
    window = jnp.concatenate([y_ref[...], halo], axis=1)
    all_ref[...] = band_product(window, bh_ref[...], bl_ref[...])
    pick_class(classes, all_ref, picked_ref, lat, columns)
    out_ref[...] = m_ref[...].astype(f32) * picked_ref[...].reshape(levels, lat, columns) * inverse


def middle_kernel(got_ref, weight_ref, innovation_ref, sum_in, inc_ref, misfit_ref, sum_ref):
    inc = jnp.sum(got_ref[...], axis=0)
    weight, innovation = weight_ref[...], innovation_ref[...]
    inc_ref[...] = inc
    misfit_ref[...] = weight * inc - innovation
    cost = 0.5 * weight * inc * inc - innovation * inc
    sum_ref[...] = sum_in[...] + jnp.sum(cost.reshape(-1, cost.shape[2]), axis=0, keepdims=True)


def weight_kernel(inverse, m_ref, misfit_ref, w_ref, right_ref, left_ref):
    w = m_ref[...].astype(f32) * misfit_ref[...] * inverse
    w_ref[...] = w
    pack_halves(w, right_ref, left_ref)


def local_kernel(classes, w_ref, x_ref, bh_ref, bl_ref, ah_ref, al_ref, out_ref, all_ref, picked_ref):
    levels, lat, columns = w_ref.shape
    rows = levels * lat
    all_ref[...] = band_product(w_ref[...].reshape(rows, columns), bh_ref[:columns], bl_ref[:columns])
    pick_class(classes, all_ref, picked_ref, lat, columns)
    part = left_product(ah_ref[...], al_ref[...], picked_ref[...])
    out_ref[...] = x_ref[...] + part.reshape(levels, lat, columns)


def adjoint_kernel(classes, fl_in, fr_in, part_ref, bh_ref, bl_ref, ah_ref, al_ref, sum_in, grad_ref, sums_ref, all_ref, picked_ref):
    levels, lat, columns = part_ref.shape
    halo = unpack_halves(fl_in[...], fr_in[...])
    all_ref[...] = band_product(halo, bh_ref[columns:], bl_ref[columns:])
    pick_class(classes, all_ref, picked_ref, lat, columns)
    edge = left_product(ah_ref[...], al_ref[...], picked_ref[...])
    grad = part_ref[...] + edge.reshape(levels, lat, columns)
    grad_ref[...] = grad
    flat = grad.reshape(-1, columns)
    square = jnp.sum(flat * flat, axis=0, keepdims=True)
    sums = jnp.concatenate([square, sum_in[...]], axis=0)
    sums_ref[...] = jnp.broadcast_to(sums[None], sums_ref.shape)


def per_device(tiles, control, members, obs_weight, innovation, scale_index):
    x = control[0]
    member = members[0]
    levels, lat, columns = x.shape
    rows = levels * lat
    groups = lax.axis_size("member")
    share = levels // groups
    cells = float(groups * rows * columns * tiles)
    inverse = float(np.float32(1.0) / np.sqrt(np.float32(groups - 1)))
    shape = jax.ShapeDtypeStruct
    half_pack = shape((levels // 2, lat, columns), f32)
    field = shape((levels, lat, columns), f32)
    square = shape((rows, rows), bf16)
    band = shape((2 * columns, CLASSES * columns), bf16)
    line = shape((1, columns), f32)
    scratch = [pltpu.VMEM((rows, CLASSES * columns), f32), pltpu.VMEM((rows, columns), f32)]
    to_right = [(i, (i + 1) % tiles) for i in range(tiles)]
    to_left = [(i, (i - 1) % tiles) for i in range(tiles)]

    first_level = lax.axis_index("member") * share
    weight_share = lax.dynamic_slice_in_dim(obs_weight, first_level, share, 0)
    innovation_share = lax.dynamic_slice_in_dim(innovation, first_level, share, 0)

    right, left = pl.pallas_call(pack_kernel, out_shape=(half_pack, half_pack), in_specs=vmem(1), out_specs=tuple(vmem(2)), compiler_params=params(), name="pack_control")(x)
    from_left = lax.ppermute(right, "tile", to_right)
    from_right = lax.ppermute(left, "tile", to_left)
    fh, fl, ah, al, bh, bl, y, half_sum = pl.pallas_call(
        prep_kernel,
        out_shape=(square, square, square, square, band, band, shape((rows, columns), f32), line),
        in_specs=[smem()] + vmem(3),
        out_specs=tuple(vmem(8)),
        scratch_shapes=[pltpu.VMEM((levels, rows), f32), pltpu.VMEM((CLASSES, lat, rows), f32)],
        compiler_params=params(),
        cost_estimate=pl.CostEstimate(flops=6 * rows * rows * columns, bytes_accessed=6 * 1024 * 1024, transcendentals=300000),
        name="operators",
    )(scale_index, scale_index.reshape(levels, 1), scale_index.reshape(1, levels), x)
    term = pl.pallas_call(
        functools.partial(forward_kernel, inverse),
        out_shape=field,
        in_specs=[smem()] + vmem(8),
        out_specs=vmem(1)[0],
        scratch_shapes=scratch,
        compiler_params=params(),
        name="forward",
    )(scale_index, from_left, from_right, y, fh, fl, bh, bl, member)
    got = lax.all_to_all(term.reshape(groups, share, lat, columns), "member", 0, 0)
    inc, misfit_share, sums = pl.pallas_call(
        middle_kernel,
        out_shape=(shape((share, lat, columns), f32), shape((share, lat, columns), f32), line),
        in_specs=vmem(4),
        out_specs=tuple(vmem(3)),
        compiler_params=params(),
        name="middle",
    )(got, weight_share, innovation_share, half_sum)
    misfit = lax.all_gather(misfit_share, "member", axis=0, tiled=True)
    w, right, left = pl.pallas_call(
        functools.partial(weight_kernel, inverse),
        out_shape=(field, half_pack, half_pack),
        in_specs=vmem(2),
        out_specs=tuple(vmem(3)),
        compiler_params=params(),
        name="weighted",
    )(member, misfit)
    from_left = lax.ppermute(right, "tile", to_right)
    from_right = lax.ppermute(left, "tile", to_left)
    part = pl.pallas_call(
        local_kernel,
        out_shape=field,
        in_specs=[smem()] + vmem(6),
        out_specs=vmem(1)[0],
        scratch_shapes=scratch,
        compiler_params=params(),
        cost_estimate=pl.CostEstimate(flops=8 * rows * rows * columns, bytes_accessed=4 * 1024 * 1024, transcendentals=0),
        name="local",
    )(scale_index, w, x, bh, bl, ah, al)
    grad, sums = pl.pallas_call(
        adjoint_kernel,
        out_shape=(field, shape((groups, 2, columns), f32)),
        in_specs=[smem()] + vmem(8),
        out_specs=tuple(vmem(2)),
        scratch_shapes=scratch,
        compiler_params=params(),
        name="adjoint",
    )(scale_index, from_left, from_right, part, bh, bl, ah, al, sums)
    sums = jnp.sum(lax.all_to_all(sums, "member", 0, 0), axis=0)
    sums = jnp.broadcast_to(sums[None], (tiles,) + sums.shape)
    sums = jnp.sum(lax.all_to_all(sums, "tile", 0, 0), axis=(0, 2)) / cells
    return inc, grad[None], sums[1], sums[0]


def solution(mesh):
    placed = (
        P("member", None, None, "tile"),
        P("member", None, None, "tile"),
        P(None, None, "tile"),
        P(None, None, "tile"),
        P(),
    )
    return jax.shard_map(
        functools.partial(per_device, mesh.shape["tile"]),
        mesh=mesh,
        in_specs=placed,
        out_specs=(P("member", None, "tile"), P("member", None, None, "tile"), P(), P()),
        check_vma=False,
    )
```

```python
import functools

import jax
import jax.numpy as jnp
import numpy as np
from jax import lax
from jax.experimental import pallas as pl
from jax.experimental.pallas import tpu as pltpu
from jax.sharding import PartitionSpec as P

CLASSES = 4
PARTS = 4
VMEM_LIMIT = 48 * 1024 * 1024
f32, bf16 = jnp.float32, jnp.bfloat16


def vmem(count):
    return [pl.BlockSpec(memory_space=pltpu.VMEM)] * count


def smem():
    return pl.BlockSpec(memory_space=pltpu.SMEM)


def params():
    return pltpu.CompilerParams(vmem_limit_bytes=VMEM_LIMIT)


def split(value):
    high = value.astype(bf16)
    low = (value - high.astype(f32)).astype(bf16)
    return high, low


def dot(a, b):
    return jnp.dot(a, b, preferred_element_type=f32)


def left_product(high, low, value):
    vhigh, vlow = split(value)
    width = value.shape[1]
    both = dot(high, jnp.concatenate([vhigh, vlow], axis=1))
    return both[:, :width] + both[:, width:] + dot(low, vhigh)


def class_product(value, hot_ref, band):
    width = value.shape[1]
    high, low = split(value)
    highs = jnp.concatenate([high * hot_ref[c] for c in range(CLASSES)], axis=1)
    lows = jnp.concatenate([low * hot_ref[c] for c in range(CLASSES)], axis=1)
    both = dot(highs, band)
    return both[:, :width] + both[:, width:] + dot(lows, band[:, :width])


def lane_is_low(shape, half):
    return lax.broadcasted_iota(jnp.int32, shape, len(shape) - 1) < half


def lane_swaps(shape, half):
    upper = lax.broadcasted_iota(jnp.int32, shape, len(shape) - 1) // half
    return (upper + lax.axis_index("tile")) % 2 == 0


def pack_halves(first, second, near_ref, far_ref, at):
    columns = first.shape[2]
    half = columns // 2
    turned = pltpu.roll(second.reshape(-1, columns), half, 1).reshape(second.shape)
    swap = lane_swaps(first.shape, half)
    near_ref[at] = jnp.where(swap, turned, first)
    far_ref[at] = jnp.where(swap, first, turned)


def unpack_halves(near, far):
    columns = near.shape[2]
    half = columns // 2
    swap = lane_swaps(near.shape, half)
    first = jnp.where(swap, near, far).reshape(-1, columns)
    second = pltpu.roll(jnp.where(swap, far, near).reshape(-1, columns), half, 1)
    return jnp.concatenate([first, second], axis=0)


def pack_kernel(x_hbm, far_ref, near_ref, x_ref, sems):
    half_levels = near_ref.shape[0]
    size = half_levels // PARTS
    copies = []
    for part in range(PARTS):
        for side in range(2):
            at = pl.ds(side * half_levels + part * size, size)
            copy = pltpu.make_async_copy(x_hbm.at[at], x_ref.at[at], sems.at[part, side])
            copy.start()
            copies.append(copy)
    for part in range(PARTS):
        copies[2 * part].wait()
        copies[2 * part + 1].wait()
        at = pl.ds(part * size, size)
        pack_halves(x_ref[at], x_ref[pl.ds(half_levels + part * size, size)], near_ref, far_ref, at)


def class_scale(c):
    return 1.0 + float(c)


def operators_kernel(
    classes, x_hbm, weight_hbm, innovation_hbm,
    fh_ref, fl_ref, ah_ref, al_ref, own_ref, halo_ref, hot_ref, y_ref, sum_ref, weight_ref, innovation_ref,
    wide_ref, pat_ref, class_ref, x_ref, sems,
):
    levels, lat, columns = x_ref.shape
    rows = levels * lat
    half = columns // 2
    share = weight_ref.shape[0]
    mine = pl.ds(lax.axis_index("member") * share, share)
    weight_copy = pltpu.make_async_copy(weight_hbm.at[mine], weight_ref, sems.at[0])
    innovation_copy = pltpu.make_async_copy(innovation_hbm.at[mine], innovation_ref, sems.at[1])
    x_copy = pltpu.make_async_copy(x_hbm, x_ref, sems.at[2])
    x_copy.start()
    weight_copy.start()
    innovation_copy.start()
    for level in range(levels):
        class_ref[pl.ds(level, 1), :] = jnp.full((1, columns), classes[level].astype(f32), f32)
    class_lines = class_ref[...]
    class_rows = jnp.broadcast_to(class_lines[:, None, :], (levels, lat, columns)).reshape(rows, columns)
    for c in range(CLASSES):
        hot_ref[c] = (class_rows == float(c)).astype(f32).astype(bf16)
    k = lax.broadcasted_iota(jnp.int32, (levels, levels), 0)
    q = lax.broadcasted_iota(jnp.int32, (levels, levels), 1)
    class_col = class_lines[:, :levels]
    class_row = jnp.sum(jnp.where(k == q, class_col, 0.0), axis=0, keepdims=True)
    scale_col = 1.0 + class_col
    scale_row = 1.0 + class_row
    spacing = (k - q).astype(f32)
    vertical = jnp.exp(-spacing * spacing / (scale_col * scale_col + scale_row * scale_row))
    which = lax.broadcasted_iota(jnp.int32, (levels, rows), 1) // lat
    spread = (which == lax.broadcasted_iota(jnp.int32, (levels, rows), 0)).astype(f32).astype(bf16)
    vh, vl = split(vertical)
    wide_ref[...] = dot(vh, spread) + dot(vl, spread)
    class_wide = dot(jnp.broadcast_to(class_row, (8, levels)).astype(bf16), spread)[:1]
    i = lax.broadcasted_iota(jnp.int32, (lat, rows), 0)
    j = lax.broadcasted_iota(jnp.int32, (lat, rows), 1) % lat
    gap = (i - j).astype(f32)
    by_column = jnp.zeros((lat, rows), f32)
    for c in range(CLASSES):
        rho = lat * class_scale(c) / 8.0
        e = np.arange(-(lat - 1), lat, dtype=np.float32)
        norm = float(np.sqrt(np.sum(np.exp(-e * e / np.float32(rho * rho)), dtype=np.float32)))
        pattern = jnp.exp(-gap * gap / (2.0 * rho * rho)) / norm
        pat_ref[c] = pattern
        by_column = jnp.where(class_wide == float(c), pattern, by_column)
    for pair in range(levels // 2):
        forward, adjoint = [], []
        for level in (2 * pair, 2 * pair + 1):
            line = wide_ref[pl.ds(level, 1), :]
            forward.append(line * pat_ref[classes[level]])
            adjoint.append(line * by_column)
        at = pl.ds(2 * pair * lat, 2 * lat)
        fh_ref[at, :], fl_ref[at, :] = split(jnp.concatenate(forward, axis=0))
        ah_ref[at, :], al_ref[at, :] = split(jnp.concatenate(adjoint, axis=0))
    d = lax.broadcasted_iota(jnp.int32, (columns, columns), 0)
    out = lax.broadcasted_iota(jnp.int32, (columns, columns), 1)
    for ref, place in ((own_ref, d), (halo_ref, jnp.where(d < half, d + columns, d - columns))):
        far = (place - out).astype(f32)
        inside = jnp.abs(far) <= half
        for c in range(CLASSES):
            sigma = half * class_scale(c) / 4.0
            e = np.arange(-half, half + 1, dtype=np.float32)
            norm = float(np.sqrt(np.sum(np.exp(-e * e / np.float32(sigma * sigma)), dtype=np.float32)))
            band = jnp.where(inside, jnp.exp(-far * far / (2.0 * sigma * sigma)) / norm, 0.0)
            at = pl.ds(c * columns, columns)
            ref[at, :columns], ref[at, columns:] = split(band)
    x_copy.wait()
    x = x_ref[...].reshape(rows, columns)
    sum_ref[...] = 0.5 * jnp.sum(x * x, axis=0, keepdims=True)
    y_ref[...] = class_product(left_product(fh_ref[...], fl_ref[...], x), hot_ref, own_ref[...])
    weight_copy.wait()
    innovation_copy.wait()


def forward_kernel(inverse, far_ref, near_ref, y_ref, fh_ref, flo_ref, halo_ref, hot_ref, m_ref, out_ref):
    levels, lat, columns = m_ref.shape
    halo = left_product(fh_ref[...], flo_ref[...], unpack_halves(near_ref[...], far_ref[...]))
    alpha = y_ref[...] + class_product(halo, hot_ref, halo_ref[...])
    out_ref[...] = m_ref[...].astype(f32) * alpha.reshape(levels, lat, columns) * inverse


def middle_kernel(got_ref, weight_ref, innovation_ref, sum_in, inc_ref, misfit_ref, sum_ref):
    inc = jnp.sum(got_ref[...], axis=0)
    weight, innovation = weight_ref[...], innovation_ref[...]
    inc_ref[...] = inc
    misfit_ref[...] = weight * inc - innovation
    cost = 0.5 * weight * inc * inc - innovation * inc
    sum_ref[...] = sum_in[...] + jnp.sum(cost.reshape(-1, cost.shape[2]), axis=0, keepdims=True)


def weight_kernel(inverse, m_ref, misfit_ref, w_ref, far_ref, near_ref):
    w = m_ref[...].astype(f32) * misfit_ref[...] * inverse
    w_ref[...] = w
    half_levels = near_ref.shape[0]
    pack_halves(w[:half_levels], w[half_levels:], near_ref, far_ref, slice(None))


def local_kernel(w_ref, x_ref, own_ref, hot_ref, ah_ref, al_ref, out_ref):
    levels, lat, columns = w_ref.shape
    rows = levels * lat
    filtered = class_product(w_ref[...].reshape(rows, columns), hot_ref, own_ref[...])
    part = left_product(ah_ref[...], al_ref[...], filtered)
    out_ref[...] = x_ref[...] + part.reshape(levels, lat, columns)


def adjoint_kernel(far_ref, near_ref, part_ref, halo_ref, hot_ref, ah_ref, al_ref, sum_in, grad_ref, sums_ref):
    levels, lat, columns = part_ref.shape
    half = columns // 2
    filtered = class_product(unpack_halves(near_ref[...], far_ref[...]), hot_ref, halo_ref[...])
    edge = left_product(ah_ref[...], al_ref[...], filtered)
    grad = part_ref[...] + edge.reshape(levels, lat, columns)
    grad_ref[...] = grad
    flat = grad.reshape(-1, columns)
    square = jnp.sum(flat * flat, axis=0, keepdims=True)
    cost = sum_in[...]
    row = jnp.where(lane_is_low(square.shape, half), square + pltpu.roll(square, half, 1), cost + pltpu.roll(cost, half, 1))
    sums_ref[...] = jnp.broadcast_to(row[None], sums_ref.shape)


def per_device(tiles, control, members, obs_weight, innovation, scale_index):
    x = control[0]
    x_hbm, weight_hbm, innovation_hbm = [pltpu.with_memory_space_constraint(v, pltpu.HBM) for v in (x, obs_weight, innovation)]
    member = members[0]
    levels, lat, columns = x.shape
    rows = levels * lat
    groups = lax.axis_size("member")
    share = levels // groups
    cells = float(groups * rows * columns * tiles)
    inverse = float(np.float32(1.0) / np.sqrt(np.float32(groups - 1)))
    half_pack = pltpu.VMEM((levels // 2, lat, columns), f32)
    field = pltpu.VMEM((levels, lat, columns), f32)
    part = pltpu.VMEM((share, lat, columns), f32)
    square = pltpu.VMEM((rows, rows), bf16)
    band = pltpu.VMEM((CLASSES * columns, 2 * columns), bf16)
    line = pltpu.VMEM((1, columns), f32)
    near_pairs = [(i, i ^ 1) for i in range(tiles)]
    far_pairs = [(i, (((i - 1) % tiles ^ 1) + 1) % tiles) for i in range(tiles)]
    hbm = [pl.BlockSpec(memory_space=pltpu.HBM)]

    far, near = pl.pallas_call(
        pack_kernel,
        out_shape=(half_pack, half_pack),
        in_specs=hbm,
        out_specs=tuple(vmem(2)),
        scratch_shapes=[pltpu.VMEM((levels, lat, columns), f32), pltpu.SemaphoreType.DMA((PARTS, 2))],
        compiler_params=params(),
        name="pack_control",
    )(x_hbm)
    far = lax.ppermute(far, "tile", far_pairs)
    near = lax.ppermute(near, "tile", near_pairs)
    fh, fl, ah, al, own, halo, hot, y, half_sum, weight_share, innovation_share = pl.pallas_call(
        operators_kernel,
        out_shape=(square, square, square, square, band, band, pltpu.VMEM((CLASSES, rows, columns), bf16), pltpu.VMEM((rows, columns), f32), line, part, part),
        in_specs=[smem()] + hbm * 3,
        out_specs=tuple(vmem(11)),
        scratch_shapes=[
            pltpu.VMEM((levels, rows), f32),
            pltpu.VMEM((CLASSES, lat, rows), f32),
            pltpu.VMEM((levels, columns), f32),
            pltpu.VMEM((levels, lat, columns), f32),
            pltpu.SemaphoreType.DMA((3,)),
        ],
        compiler_params=params(),
        cost_estimate=pl.CostEstimate(flops=6 * rows * rows * columns, bytes_accessed=6 * 1024 * 1024, transcendentals=300000),
        name="operators",
    )(scale_index, x_hbm, weight_hbm, innovation_hbm)
    term = pl.pallas_call(
        functools.partial(forward_kernel, inverse),
        out_shape=field,
        in_specs=vmem(8),
        out_specs=vmem(1)[0],
        compiler_params=params(),
        name="forward",
    )(far, near, y, fh, fl, halo, hot, member)
    got = lax.all_to_all(term.reshape(groups, share, lat, columns), "member", 0, 0)
    inc, misfit_share, sums = pl.pallas_call(
        middle_kernel,
        out_shape=(part, part, line),
        in_specs=vmem(4),
        out_specs=tuple(vmem(3)),
        compiler_params=params(),
        name="middle",
    )(got, weight_share, innovation_share, half_sum)
    misfit = lax.all_gather(misfit_share, "member", axis=0, tiled=True)
    w, far, near = pl.pallas_call(
        functools.partial(weight_kernel, inverse),
        out_shape=(field, half_pack, half_pack),
        in_specs=vmem(2),
        out_specs=tuple(vmem(3)),
        compiler_params=params(),
        name="weighted",
    )(member, misfit)
    far = lax.ppermute(far, "tile", far_pairs)
    near = lax.ppermute(near, "tile", near_pairs)
    inner = pl.pallas_call(
        local_kernel,
        out_shape=field,
        in_specs=vmem(6),
        out_specs=vmem(1)[0],
        compiler_params=params(),
        cost_estimate=pl.CostEstimate(flops=8 * rows * rows * columns, bytes_accessed=4 * 1024 * 1024, transcendentals=0),
        name="local",
    )(w, x, own, hot, ah, al)
    grad, sums = pl.pallas_call(
        adjoint_kernel,
        out_shape=(field, pltpu.VMEM((groups, 1, columns), f32)),
        in_specs=vmem(8),
        out_specs=tuple(vmem(2)),
        compiler_params=params(),
        name="adjoint",
    )(far, near, inner, halo, hot, ah, al, sums)
    sums = jnp.sum(lax.all_to_all(sums, "member", 0, 0), axis=0)
    sums = jnp.broadcast_to(sums[None], (tiles,) + sums.shape)
    sums = jnp.sum(lax.all_to_all(sums, "tile", 0, 0), axis=0)
    sums = jnp.sum(sums.reshape(2, columns // 2), axis=1) / cells
    return inc, grad[None], sums[1], sums[0]


def solution(mesh):
    placed = (
        P("member", None, None, "tile"),
        P("member", None, None, "tile"),
        P(None, None, "tile"),
        P(None, None, "tile"),
        P(),
    )
    return jax.shard_map(
        functools.partial(per_device, mesh.shape["tile"]),
        mesh=mesh,
        in_specs=placed,
        out_specs=(P("member", None, "tile"), P("member", None, None, "tile"), P(), P()),
        check_vma=False,
    )
```

```python
import functools

import jax
import jax.numpy as jnp
import numpy as np
from jax import lax
from jax.experimental import pallas as pl
from jax.experimental.pallas import tpu as pltpu
from jax.sharding import PartitionSpec as P

CLASSES = 4
PARTS = 4
VMEM_LIMIT = 48 * 1024 * 1024
f32, bf16 = jnp.float32, jnp.bfloat16


def vmem(count):
    return [pl.BlockSpec(memory_space=pltpu.VMEM)] * count


def smem():
    return pl.BlockSpec(memory_space=pltpu.SMEM)


def params():
    return pltpu.CompilerParams(vmem_limit_bytes=VMEM_LIMIT)


def split(value):
    high = value.astype(bf16)
    low = (value - high.astype(f32)).astype(bf16)
    return high, low


def dot(a, b):
    return jnp.dot(a, b, preferred_element_type=f32)


def left_product(high, low, value):
    vhigh, vlow = split(value)
    width = value.shape[1]
    both = dot(high, jnp.concatenate([vhigh, vlow], axis=1))
    return both[:, :width] + both[:, width:] + dot(low, vhigh)


def class_product(value, hot_ref, band):
    width = value.shape[1]
    high, low = split(value)
    highs = jnp.concatenate([high * hot_ref[c] for c in range(CLASSES)], axis=1)
    lows = jnp.concatenate([low * hot_ref[c] for c in range(CLASSES)], axis=1)
    both = dot(highs, band)
    return both[:, :width] + both[:, width:] + dot(lows, band[:, :width])


def lane_is_low(shape, half):
    return lax.broadcasted_iota(jnp.int32, shape, len(shape) - 1) < half


def lane_swaps(shape, half):
    upper = lax.broadcasted_iota(jnp.int32, shape, len(shape) - 1) // half
    return (upper + lax.axis_index("tile")) % 2 == 0


def pack_halves(first, second, near_ref, far_ref, at):
    columns = first.shape[2]
    half = columns // 2
    turned = pltpu.roll(second.reshape(-1, columns), half, 1).reshape(second.shape)
    swap = lane_swaps(first.shape, half)
    near_ref[at] = jnp.where(swap, turned, first)
    far_ref[at] = jnp.where(swap, first, turned)


def unpack_halves(near, far):
    columns = near.shape[2]
    half = columns // 2
    swap = lane_swaps(near.shape, half)
    first = jnp.where(swap, near, far).reshape(-1, columns)
    second = pltpu.roll(jnp.where(swap, far, near).reshape(-1, columns), half, 1)
    return jnp.concatenate([first, second], axis=0)


def pack_kernel(x_hbm, far_ref, near_ref, x_ref, sems):
    half_levels = near_ref.shape[0]
    size = half_levels // PARTS
    copies = []
    for part in range(PARTS):
        for side in range(2):
            at = pl.ds(side * half_levels + part * size, size)
            copy = pltpu.make_async_copy(x_hbm.at[at], x_ref.at[at], sems.at[part, side])
            copy.start()
            copies.append(copy)
    for part in range(PARTS):
        copies[2 * part].wait()
        copies[2 * part + 1].wait()
        at = pl.ds(part * size, size)
        pack_halves(x_ref[at], x_ref[pl.ds(half_levels + part * size, size)], near_ref, far_ref, at)


def class_scale(c):
    return 1.0 + float(c)


def operators_kernel(
    classes, x_ref, weight_hbm, innovation_hbm,
    fh_ref, fl_ref, wide_ref, mix_ref, own_ref, halo_ref, hot_ref, y_ref, sum_ref, weight_ref, innovation_ref,
    class_ref, class_rows_ref, sems,
):
    levels, lat, columns = x_ref.shape
    rows = levels * lat
    half = columns // 2
    share = weight_ref.shape[0]
    mine = pl.ds(lax.axis_index("member") * share, share)
    weight_copy = pltpu.make_async_copy(weight_hbm.at[mine], weight_ref, sems.at[0])
    innovation_copy = pltpu.make_async_copy(innovation_hbm.at[mine], innovation_ref, sems.at[1])
    weight_copy.start()
    innovation_copy.start()
    for level in range(levels):
        class_ref[pl.ds(level, 1), :] = jnp.full((1, columns), classes[level].astype(f32), f32)
    class_lines = class_ref[...]
    class_rows = jnp.broadcast_to(class_lines[:, None, :], (levels, lat, columns)).reshape(rows, columns)
    class_rows_ref[...] = class_rows
    for c in range(CLASSES):
        hot_ref[c] = (class_rows == float(c)).astype(f32).astype(bf16)
    k = lax.broadcasted_iota(jnp.int32, (levels, levels), 0)
    q = lax.broadcasted_iota(jnp.int32, (levels, levels), 1)
    class_col = class_lines[:, :levels]
    class_row = jnp.sum(jnp.where(k == q, class_col, 0.0), axis=0, keepdims=True)
    scale_col = 1.0 + class_col
    scale_row = 1.0 + class_row
    spacing = (k - q).astype(f32)
    vertical = jnp.exp(-spacing * spacing / (scale_col * scale_col + scale_row * scale_row))
    ahead = lax.broadcasted_iota(jnp.int32, (levels, rows), 1) - lat * lax.broadcasted_iota(jnp.int32, (levels, rows), 0)
    spread = ((ahead >= 0) & (ahead < lat)).astype(f32).astype(bf16)
    vh, vl = split(vertical)
    wide_ref[...] = dot(vh, spread) + dot(vl, spread)
    class_wide = dot(jnp.broadcast_to(class_row, (8, levels)).astype(bf16), spread)[:1]
    i = lax.broadcasted_iota(jnp.int32, (lat, rows), 0)
    j = lax.broadcasted_iota(jnp.int32, (lat, rows), 1) & (lat - 1)
    gap = (i - j).astype(f32)
    patterns = []
    mix = jnp.zeros((lat, rows), f32)
    for c in range(CLASSES):
        rho = lat * class_scale(c) / 8.0
        e = np.arange(-(lat - 1), lat, dtype=np.float32)
        norm = float(np.sqrt(np.sum(np.exp(-e * e / np.float32(rho * rho)), dtype=np.float32)))
        patterns.append(jnp.exp(-gap * gap / (2.0 * rho * rho)) / norm)
        mix = jnp.where(class_wide == float(c), patterns[c], mix)
    mix_ref[...] = mix
    for pair in range(levels // 2):
        both = []
        for level in (2 * pair, 2 * pair + 1):
            kind = class_rows_ref[pl.ds(level * lat, lat), :1]
            pattern = patterns[CLASSES - 1]
            for c in range(CLASSES - 1):
                pattern = jnp.where(kind == float(c), patterns[c], pattern)
            both.append(wide_ref[pl.ds(level, 1), :] * pattern)
        at = pl.ds(2 * pair * lat, 2 * lat)
        fh_ref[at, :], fl_ref[at, :] = split(jnp.concatenate(both, axis=0))
    d = lax.broadcasted_iota(jnp.int32, (columns, columns), 0)
    out = lax.broadcasted_iota(jnp.int32, (columns, columns), 1)
    for ref, place in ((own_ref, d), (halo_ref, jnp.where(d < half, d + columns, d - columns))):
        far = (place - out).astype(f32)
        inside = jnp.abs(far) <= half
        for c in range(CLASSES):
            sigma = half * class_scale(c) / 4.0
            e = np.arange(-half, half + 1, dtype=np.float32)
            norm = float(np.sqrt(np.sum(np.exp(-e * e / np.float32(sigma * sigma)), dtype=np.float32)))
            band = jnp.where(inside, jnp.exp(-far * far / (2.0 * sigma * sigma)) / norm, 0.0)
            at = pl.ds(c * columns, columns)
            ref[at, :columns], ref[at, columns:] = split(band)
    x = x_ref[...].reshape(rows, columns)
    sum_ref[...] = 0.5 * jnp.sum(x * x, axis=0, keepdims=True)
    y_ref[...] = class_product(left_product(fh_ref[...], fl_ref[...], x), hot_ref, own_ref[...])
    weight_copy.wait()
    innovation_copy.wait()


def forward_kernel(inverse, far_ref, near_ref, y_ref, fh_ref, flo_ref, halo_ref, hot_ref, m_ref, mine_ref, other_ref):
    levels, lat, columns = m_ref.shape
    halo = left_product(fh_ref[...], flo_ref[...], unpack_halves(near_ref[...], far_ref[...]))
    alpha = y_ref[...] + class_product(halo, hot_ref, halo_ref[...])
    term = m_ref[...].astype(f32) * alpha.reshape(levels, lat, columns) * inverse
    chips, share = mine_ref.shape[:2]
    term = term.reshape(chips, 2, share, lat, columns)
    even = lax.axis_index("member") % 2 == 0
    mine_ref[...] = jnp.where(even, term[:, 0], term[:, 1])
    other_ref[...] = jnp.where(even, term[:, 1], term[:, 0])


def add_kernel(a_ref, b_ref, out_ref):
    out_ref[...] = a_ref[...] + b_ref[...]


def middle_kernel(got_ref, weight_ref, innovation_ref, sum_in, inc_ref, misfit_ref, sum_ref):
    inc = jnp.sum(got_ref[...], axis=0)
    weight, innovation = weight_ref[...], innovation_ref[...]
    inc_ref[...] = inc
    misfit_ref[...] = jnp.broadcast_to((weight * inc - innovation)[None], misfit_ref.shape)
    cost = 0.5 * weight * inc * inc - innovation * inc
    sum_ref[...] = sum_in[...] + jnp.sum(cost.reshape(-1, cost.shape[2]), axis=0, keepdims=True)


def weight_kernel(inverse, m_ref, mine_ref, other_ref, w_ref, far_ref, near_ref):
    levels, lat, columns = m_ref.shape
    mine, other = mine_ref[...], other_ref[...]
    even = lax.axis_index("member") % 2 == 0
    misfit = jnp.stack([jnp.where(even, mine, other), jnp.where(even, other, mine)], axis=1)
    w = m_ref[...].astype(f32) * misfit.reshape(levels, lat, columns) * inverse
    w_ref[...] = w
    half_levels = near_ref.shape[0]
    pack_halves(w[:half_levels], w[half_levels:], near_ref, far_ref, slice(None))


def local_kernel(w_ref, x_ref, own_ref, hot_ref, wide_ref, mix_ref, out_ref, ah_ref, al_ref):
    levels, lat, columns = w_ref.shape
    rows = levels * lat
    mix = mix_ref[...]
    for pair in range(levels // 2):
        both = [wide_ref[pl.ds(level, 1), :] * mix for level in (2 * pair, 2 * pair + 1)]
        at = pl.ds(2 * pair * lat, 2 * lat)
        ah_ref[at, :], al_ref[at, :] = split(jnp.concatenate(both, axis=0))
    filtered = class_product(w_ref[...].reshape(rows, columns), hot_ref, own_ref[...])
    part = left_product(ah_ref[...], al_ref[...], filtered)
    out_ref[...] = x_ref[...] + part.reshape(levels, lat, columns)


def adjoint_kernel(far_ref, near_ref, part_ref, halo_ref, hot_ref, ah_ref, al_ref, sum_in, grad_ref, sums_ref):
    levels, lat, columns = part_ref.shape
    half = columns // 2
    filtered = class_product(unpack_halves(near_ref[...], far_ref[...]), hot_ref, halo_ref[...])
    edge = left_product(ah_ref[...], al_ref[...], filtered)
    grad = part_ref[...] + edge.reshape(levels, lat, columns)
    grad_ref[...] = grad
    flat = grad.reshape(-1, columns)
    square = jnp.sum(flat * flat, axis=0, keepdims=True)
    cost = sum_in[...]
    row = jnp.where(lane_is_low(square.shape, half), square + pltpu.roll(square, half, 1), cost + pltpu.roll(cost, half, 1))
    sums_ref[...] = jnp.broadcast_to(row[None], sums_ref.shape)


def per_device(tiles, control, members, obs_weight, innovation, scale_index):
    x = control[0]
    in_hbm = (x, obs_weight, innovation, scale_index)
    x_hbm, weight_hbm, innovation_hbm, classes = [pltpu.with_memory_space_constraint(v, pltpu.HBM) for v in in_hbm]
    member = members[0]
    levels, lat, columns = x.shape
    rows = levels * lat
    groups = lax.axis_size("member")
    share = levels // groups
    cells = float(groups * rows * columns * tiles)
    inverse = float(np.float32(1.0) / np.sqrt(np.float32(groups - 1)))
    half_pack = pltpu.VMEM((levels // 2, lat, columns), f32)
    field = pltpu.VMEM((levels, lat, columns), f32)
    part = pltpu.VMEM((share, lat, columns), f32)
    square = pltpu.VMEM((rows, rows), bf16)
    band = pltpu.VMEM((CLASSES * columns, 2 * columns), bf16)
    line = pltpu.VMEM((1, columns), f32)
    chips = [list(range(core, groups, 2)) for core in range(2)]
    partners = [(i, i ^ 1) for i in range(groups)]
    near_pairs = [(i, i ^ 1) for i in range(tiles)]
    far_pairs = [(i, (((i - 1) % tiles ^ 1) + 1) % tiles) for i in range(tiles)]
    hbm = [pl.BlockSpec(memory_space=pltpu.HBM)]

    far, near, x_near = pl.pallas_call(
        pack_kernel,
        out_shape=(half_pack, half_pack, field),
        in_specs=hbm,
        out_specs=tuple(vmem(3)),
        scratch_shapes=[pltpu.SemaphoreType.DMA((PARTS, 2))],
        compiler_params=params(),
        name="pack_control",
    )(x_hbm)
    far = lax.ppermute(far, "tile", far_pairs)
    near = lax.ppermute(near, "tile", near_pairs)
    fh, fl, wide, mix, own, halo, hot, y, half_sum, weight_share, innovation_share = pl.pallas_call(
        operators_kernel,
        out_shape=(square, square, pltpu.VMEM((levels, rows), f32), pltpu.VMEM((lat, rows), f32), band, band, pltpu.VMEM((CLASSES, rows, columns), bf16), pltpu.VMEM((rows, columns), f32), line, part, part),
        in_specs=[smem()] + vmem(1) + hbm * 2,
        out_specs=tuple(vmem(11)),
        scratch_shapes=[
            pltpu.VMEM((levels, columns), f32),
            pltpu.VMEM((rows, columns), f32),
            pltpu.SemaphoreType.DMA((2,)),
        ],
        compiler_params=params(),
        cost_estimate=pl.CostEstimate(flops=6 * rows * rows * columns, bytes_accessed=6 * 1024 * 1024, transcendentals=300000),
        name="operators",
    )(classes, x_near, weight_hbm, innovation_hbm)
    half_term = pltpu.VMEM((groups // 2, share, lat, columns), f32)
    mine, other = pl.pallas_call(
        functools.partial(forward_kernel, inverse),
        out_shape=(half_term, half_term),
        in_specs=vmem(8),
        out_specs=tuple(vmem(2)),
        compiler_params=params(),
        name="forward",
    )(far, near, y, fh, fl, halo, hot, member)
    other = lax.ppermute(other, "member", partners)
    both = pl.pallas_call(add_kernel, out_shape=half_term, in_specs=vmem(2), out_specs=vmem(1)[0], compiler_params=params(), name="add_cores")(mine, other)
    got = lax.all_to_all(both, "member", 0, 0, axis_index_groups=chips)
    inc, misfit_share, sums = pl.pallas_call(
        middle_kernel,
        out_shape=(part, pltpu.VMEM((groups // 2, share, lat, columns), f32), line),
        in_specs=vmem(4),
        out_specs=tuple(vmem(3)),
        compiler_params=params(),
        name="middle",
    )(got, weight_share, innovation_share, half_sum)
    misfit_mine = lax.all_to_all(misfit_share, "member", 0, 0, axis_index_groups=chips)
    misfit_other = lax.ppermute(misfit_mine, "member", partners)
    w, far, near = pl.pallas_call(
        functools.partial(weight_kernel, inverse),
        out_shape=(field, half_pack, half_pack),
        in_specs=vmem(3),
        out_specs=tuple(vmem(3)),
        compiler_params=params(),
        name="weighted",
    )(member, misfit_mine, misfit_other)
    far = lax.ppermute(far, "tile", far_pairs)
    near = lax.ppermute(near, "tile", near_pairs)
    inner, ah, al = pl.pallas_call(
        local_kernel,
        out_shape=(field, square, square),
        in_specs=vmem(6),
        out_specs=tuple(vmem(3)),
        compiler_params=params(),
        cost_estimate=pl.CostEstimate(flops=8 * rows * rows * columns, bytes_accessed=4 * 1024 * 1024, transcendentals=0),
        name="local",
    )(w, x, own, hot, wide, mix)
    grad, sums = pl.pallas_call(
        adjoint_kernel,
        out_shape=(field, pltpu.VMEM((groups, 1, columns), f32)),
        in_specs=vmem(8),
        out_specs=tuple(vmem(2)),
        compiler_params=params(),
        name="adjoint",
    )(far, near, inner, halo, hot, ah, al, sums)
    sums = jnp.sum(lax.all_to_all(sums, "member", 0, 0), axis=0)
    sums = jnp.broadcast_to(sums[None], (tiles,) + sums.shape)
    sums = jnp.sum(lax.all_to_all(sums, "tile", 0, 0), axis=0)
    sums = jnp.sum(sums.reshape(2, columns // 2), axis=1) / cells
    return inc, grad[None], sums[1], sums[0]


def solution(mesh):
    placed = (
        P("member", None, None, "tile"),
        P("member", None, None, "tile"),
        P(None, None, "tile"),
        P(None, None, "tile"),
        P(),
    )
    return jax.shard_map(
        functools.partial(per_device, mesh.shape["tile"]),
        mesh=mesh,
        in_specs=placed,
        out_specs=(P("member", None, "tile"), P("member", None, None, "tile"), P(), P()),
        check_vma=False,
    )
```

```python
import functools

import jax
import jax.numpy as jnp
import numpy as np
from jax import lax
from jax.experimental import pallas as pl
from jax.experimental.pallas import tpu as pltpu
from jax.sharding import PartitionSpec as P

CLASSES = 4
PARTS = 4
VMEM_LIMIT = 48 * 1024 * 1024
f32, bf16 = jnp.float32, jnp.bfloat16


def vmem(count):
    return [pl.BlockSpec(memory_space=pltpu.VMEM)] * count


def smem():
    return pl.BlockSpec(memory_space=pltpu.SMEM)


def params():
    return pltpu.CompilerParams(vmem_limit_bytes=VMEM_LIMIT)


def split(value):
    high = value.astype(bf16)
    low = (value - high.astype(f32)).astype(bf16)
    return high, low


def dot(a, b):
    return jnp.dot(a, b, preferred_element_type=f32)


def left_product(high, low, value):
    vhigh, vlow = split(value)
    width = value.shape[1]
    both = dot(high, jnp.concatenate([vhigh, vlow], axis=1))
    return both[:, :width] + both[:, width:] + dot(low, vhigh)


def class_product(value, hot_ref, band):
    width = value.shape[1]
    high, low = split(value)
    highs = jnp.concatenate([high * hot_ref[c] for c in range(CLASSES)], axis=1)
    lows = jnp.concatenate([low * hot_ref[c] for c in range(CLASSES)], axis=1)
    both = dot(highs, band)
    return both[:, :width] + both[:, width:] + dot(lows, band[:, :width])


def lane_is_low(shape, half):
    return lax.broadcasted_iota(jnp.int32, shape, len(shape) - 1) < half


def lane_swaps(shape, half):
    upper = lax.broadcasted_iota(jnp.int32, shape, len(shape) - 1) // half
    return (upper + lax.axis_index("tile")) % 2 == 0


def pack_halves(first, second, near_ref, far_ref, at):
    columns = first.shape[2]
    half = columns // 2
    turned = pltpu.roll(second.reshape(-1, columns), half, 1).reshape(second.shape)
    swap = lane_swaps(first.shape, half)
    near_ref[at] = jnp.where(swap, turned, first)
    far_ref[at] = jnp.where(swap, first, turned)


def unpack_halves(near, far):
    columns = near.shape[2]
    half = columns // 2
    swap = lane_swaps(near.shape, half)
    first = jnp.where(swap, near, far).reshape(-1, columns)
    second = pltpu.roll(jnp.where(swap, far, near).reshape(-1, columns), half, 1)
    return jnp.concatenate([first, second], axis=0)


def pack_kernel(x_hbm, far_ref, near_ref, x_ref, sems):
    half_levels = near_ref.shape[0]
    size = half_levels // PARTS
    copies = []
    for part in range(PARTS):
        for side in range(2):
            at = pl.ds(side * half_levels + part * size, size)
            copy = pltpu.make_async_copy(x_hbm.at[at], x_ref.at[at], sems.at[part, side])
            copy.start()
            copies.append(copy)
    for part in range(PARTS):
        copies[2 * part].wait()
        copies[2 * part + 1].wait()
        at = pl.ds(part * size, size)
        pack_halves(x_ref[at], x_ref[pl.ds(half_levels + part * size, size)], near_ref, far_ref, at)


def class_scale(c):
    return 1.0 + float(c)


def operators_kernel(
    classes, x_ref, weight_hbm, innovation_hbm,
    fh_ref, fl_ref, wide_ref, mix_ref, own_ref, halo_ref, hot_ref, y_ref, sum_ref, weight_ref, innovation_ref,
    class_ref, class_rows_ref, sems,
):
    levels, lat, columns = x_ref.shape
    rows = levels * lat
    half = columns // 2
    share = weight_ref.shape[0]
    mine = pl.ds(lax.axis_index("member") * share, share)
    weight_copy = pltpu.make_async_copy(weight_hbm.at[mine], weight_ref, sems.at[0])
    innovation_copy = pltpu.make_async_copy(innovation_hbm.at[mine], innovation_ref, sems.at[1])
    weight_copy.start()
    innovation_copy.start()
    for level in range(levels):
        class_ref[pl.ds(level, 1), :] = jnp.full((1, columns), classes[level].astype(f32), f32)
    class_lines = class_ref[...]
    class_rows = jnp.broadcast_to(class_lines[:, None, :], (levels, lat, columns)).reshape(rows, columns)
    class_rows_ref[...] = class_rows
    for c in range(CLASSES):
        hot_ref[c] = (class_rows == float(c)).astype(f32).astype(bf16)
    k = lax.broadcasted_iota(jnp.int32, (levels, levels), 0)
    q = lax.broadcasted_iota(jnp.int32, (levels, levels), 1)
    class_col = class_lines[:, :levels]
    class_row = jnp.sum(jnp.where(k == q, class_col, 0.0), axis=0, keepdims=True)
    scale_col = 1.0 + class_col
    scale_row = 1.0 + class_row
    spacing = (k - q).astype(f32)
    vertical = jnp.exp(-spacing * spacing / (scale_col * scale_col + scale_row * scale_row))
    ahead = lax.broadcasted_iota(jnp.int32, (levels, rows), 1) - lat * lax.broadcasted_iota(jnp.int32, (levels, rows), 0)
    spread = ((ahead >= 0) & (ahead < lat)).astype(f32).astype(bf16)
    vh, vl = split(vertical)
    wide_ref[...] = dot(vh, spread) + dot(vl, spread)
    class_wide = dot(jnp.broadcast_to(class_row, (8, levels)).astype(bf16), spread)[:1]
    i = lax.broadcasted_iota(jnp.int32, (lat, rows), 0)
    j = lax.broadcasted_iota(jnp.int32, (lat, rows), 1) & (lat - 1)
    gap = (i - j).astype(f32)
    patterns = []
    mix = jnp.zeros((lat, rows), f32)
    for c in range(CLASSES):
        rho = lat * class_scale(c) / 8.0
        e = np.arange(-(lat - 1), lat, dtype=np.float32)
        norm = float(np.sqrt(np.sum(np.exp(-e * e / np.float32(rho * rho)), dtype=np.float32)))
        patterns.append(jnp.exp(-gap * gap / (2.0 * rho * rho)) / norm)
        mix = jnp.where(class_wide == float(c), patterns[c], mix)
    mix_ref[...] = mix
    for pair in range(levels // 2):
        both = []
        for level in (2 * pair, 2 * pair + 1):
            kind = class_rows_ref[pl.ds(level * lat, lat), :1]
            pattern = patterns[CLASSES - 1]
            for c in range(CLASSES - 1):
                pattern = jnp.where(kind == float(c), patterns[c], pattern)
            both.append(wide_ref[pl.ds(level, 1), :] * pattern)
        at = pl.ds(2 * pair * lat, 2 * lat)
        fh_ref[at, :], fl_ref[at, :] = split(jnp.concatenate(both, axis=0))
    d = lax.broadcasted_iota(jnp.int32, (columns, columns), 0)
    out = lax.broadcasted_iota(jnp.int32, (columns, columns), 1)
    for ref, place in ((own_ref, d), (halo_ref, jnp.where(d < half, d + columns, d - columns))):
        far = (place - out).astype(f32)
        inside = jnp.abs(far) <= half
        for c in range(CLASSES):
            sigma = half * class_scale(c) / 4.0
            e = np.arange(-half, half + 1, dtype=np.float32)
            norm = float(np.sqrt(np.sum(np.exp(-e * e / np.float32(sigma * sigma)), dtype=np.float32)))
            band = jnp.where(inside, jnp.exp(-far * far / (2.0 * sigma * sigma)) / norm, 0.0)
            at = pl.ds(c * columns, columns)
            ref[at, :columns], ref[at, columns:] = split(band)
    x = x_ref[...].reshape(rows, columns)
    sum_ref[...] = 0.5 * jnp.sum(x * x, axis=0, keepdims=True)
    y_ref[...] = class_product(left_product(fh_ref[...], fl_ref[...], x), hot_ref, own_ref[...])
    weight_copy.wait()
    innovation_copy.wait()


def forward_kernel(inverse, far_ref, near_ref, y_ref, fh_ref, flo_ref, halo_ref, hot_ref, m_ref, mine_ref, other_ref):
    levels, lat, columns = m_ref.shape
    halo = left_product(fh_ref[...], flo_ref[...], unpack_halves(near_ref[...], far_ref[...]))
    alpha = y_ref[...] + class_product(halo, hot_ref, halo_ref[...])
    term = m_ref[...].astype(f32) * alpha.reshape(levels, lat, columns) * inverse
    chips, share = mine_ref.shape[:2]
    term = term.reshape(chips, 2, share, lat, columns)
    even = lax.axis_index("member") % 2 == 0
    mine_ref[...] = jnp.where(even, term[:, 0], term[:, 1])
    other_ref[...] = jnp.where(even, term[:, 1], term[:, 0])


def add_kernel(mine_ref, sent_ref, out_ref):
    out_ref[...] = mine_ref[...] + sent_ref[1 - lax.axis_index("member") % 2]


def middle_kernel(got_ref, weight_ref, innovation_ref, sum_in, inc_ref, misfit_ref, sum_ref):
    inc = jnp.sum(got_ref[...], axis=0)
    weight, innovation = weight_ref[...], innovation_ref[...]
    inc_ref[...] = inc
    misfit_ref[...] = jnp.broadcast_to((weight * inc - innovation)[None], misfit_ref.shape)
    cost = 0.5 * weight * inc * inc - innovation * inc
    sum_ref[...] = sum_in[...] + jnp.sum(cost.reshape(-1, cost.shape[2]), axis=0, keepdims=True)


def weight_kernel(inverse, m_ref, both_ref, w_ref, far_ref, near_ref):
    levels, lat, columns = m_ref.shape
    misfit = jnp.stack([both_ref[0], both_ref[1]], axis=1)
    w = m_ref[...].astype(f32) * misfit.reshape(levels, lat, columns) * inverse
    w_ref[...] = w
    half_levels = near_ref.shape[0]
    pack_halves(w[:half_levels], w[half_levels:], near_ref, far_ref, slice(None))


def local_kernel(w_ref, x_ref, own_ref, hot_ref, wide_ref, mix_ref, out_ref, ah_ref, al_ref):
    levels, lat, columns = w_ref.shape
    rows = levels * lat
    mix = mix_ref[...]
    for pair in range(levels // 2):
        both = [wide_ref[pl.ds(level, 1), :] * mix for level in (2 * pair, 2 * pair + 1)]
        at = pl.ds(2 * pair * lat, 2 * lat)
        ah_ref[at, :], al_ref[at, :] = split(jnp.concatenate(both, axis=0))
    filtered = class_product(w_ref[...].reshape(rows, columns), hot_ref, own_ref[...])
    part = left_product(ah_ref[...], al_ref[...], filtered)
    out_ref[...] = x_ref[...] + part.reshape(levels, lat, columns)


def adjoint_kernel(far_ref, near_ref, part_ref, halo_ref, hot_ref, ah_ref, al_ref, sum_in, grad_ref, sums_ref):
    levels, lat, columns = part_ref.shape
    half = columns // 2
    filtered = class_product(unpack_halves(near_ref[...], far_ref[...]), hot_ref, halo_ref[...])
    edge = left_product(ah_ref[...], al_ref[...], filtered)
    grad = part_ref[...] + edge.reshape(levels, lat, columns)
    grad_ref[...] = grad
    flat = grad.reshape(-1, columns)
    square = jnp.sum(flat * flat, axis=0, keepdims=True)
    cost = sum_in[...]
    row = jnp.where(lane_is_low(square.shape, half), square + pltpu.roll(square, half, 1), cost + pltpu.roll(cost, half, 1))
    sums_ref[...] = jnp.broadcast_to(row[None], sums_ref.shape)


def per_device(tiles, control, members, obs_weight, innovation, scale_index):
    x = control[0]
    in_hbm = (x, obs_weight, innovation, scale_index)
    x_hbm, weight_hbm, innovation_hbm, classes = [pltpu.with_memory_space_constraint(v, pltpu.HBM) for v in in_hbm]
    member = members[0]
    levels, lat, columns = x.shape
    rows = levels * lat
    groups = lax.axis_size("member")
    share = levels // groups
    cells = float(groups * rows * columns * tiles)
    inverse = float(np.float32(1.0) / np.sqrt(np.float32(groups - 1)))
    half_pack = pltpu.VMEM((levels // 2, lat, columns), f32)
    field = pltpu.VMEM((levels, lat, columns), f32)
    part = pltpu.VMEM((share, lat, columns), f32)
    square = pltpu.VMEM((rows, rows), bf16)
    band = pltpu.VMEM((CLASSES * columns, 2 * columns), bf16)
    line = pltpu.VMEM((1, columns), f32)
    chips = [list(range(core, groups, 2)) for core in range(2)]
    cores = [[i, i + 1] for i in range(0, groups, 2)]
    near_pairs = [(i, i ^ 1) for i in range(tiles)]
    far_pairs = [(i, (((i - 1) % tiles ^ 1) + 1) % tiles) for i in range(tiles)]
    hbm = [pl.BlockSpec(memory_space=pltpu.HBM)]

    far, near, x_near = pl.pallas_call(
        pack_kernel,
        out_shape=(half_pack, half_pack, field),
        in_specs=hbm,
        out_specs=tuple(vmem(3)),
        scratch_shapes=[pltpu.SemaphoreType.DMA((PARTS, 2))],
        compiler_params=params(),
        name="pack_control",
    )(x_hbm)
    far = lax.ppermute(far, "tile", far_pairs)
    near = lax.ppermute(near, "tile", near_pairs)
    fh, fl, wide, mix, own, halo, hot, y, half_sum, weight_share, innovation_share = pl.pallas_call(
        operators_kernel,
        out_shape=(square, square, pltpu.VMEM((levels, rows), f32), pltpu.VMEM((lat, rows), f32), band, band, pltpu.VMEM((CLASSES, rows, columns), bf16), pltpu.VMEM((rows, columns), f32), line, part, part),
        in_specs=[smem()] + vmem(1) + hbm * 2,
        out_specs=tuple(vmem(11)),
        scratch_shapes=[
            pltpu.VMEM((levels, columns), f32),
            pltpu.VMEM((rows, columns), f32),
            pltpu.SemaphoreType.DMA((2,)),
        ],
        compiler_params=params(),
        cost_estimate=pl.CostEstimate(flops=6 * rows * rows * columns, bytes_accessed=6 * 1024 * 1024, transcendentals=300000),
        name="operators",
    )(classes, x_near, weight_hbm, innovation_hbm)
    half_term = pltpu.VMEM((groups // 2, share, lat, columns), f32)
    mine, other = pl.pallas_call(
        functools.partial(forward_kernel, inverse),
        out_shape=(half_term, half_term),
        in_specs=vmem(8),
        out_specs=tuple(vmem(2)),
        compiler_params=params(),
        name="forward",
    )(far, near, y, fh, fl, halo, hot, member)
    sent = lax.all_gather(other, "member", axis_index_groups=cores)
    both = pl.pallas_call(add_kernel, out_shape=half_term, in_specs=vmem(2), out_specs=vmem(1)[0], compiler_params=params(), name="add_cores")(mine, sent)
    got = lax.all_to_all(both, "member", 0, 0, axis_index_groups=chips)
    inc, misfit_share, sums = pl.pallas_call(
        middle_kernel,
        out_shape=(part, pltpu.VMEM((groups // 2, share, lat, columns), f32), line),
        in_specs=vmem(4),
        out_specs=tuple(vmem(3)),
        compiler_params=params(),
        name="middle",
    )(got, weight_share, innovation_share, half_sum)
    misfit_mine = lax.all_to_all(misfit_share, "member", 0, 0, axis_index_groups=chips)
    misfit = lax.all_gather(misfit_mine, "member", axis_index_groups=cores)
    w, far, near = pl.pallas_call(
        functools.partial(weight_kernel, inverse),
        out_shape=(field, half_pack, half_pack),
        in_specs=vmem(2),
        out_specs=tuple(vmem(3)),
        compiler_params=params(),
        name="weighted",
    )(member, misfit)
    far = lax.ppermute(far, "tile", far_pairs)
    near = lax.ppermute(near, "tile", near_pairs)
    inner, ah, al = pl.pallas_call(
        local_kernel,
        out_shape=(field, square, square),
        in_specs=vmem(6),
        out_specs=tuple(vmem(3)),
        compiler_params=params(),
        cost_estimate=pl.CostEstimate(flops=8 * rows * rows * columns, bytes_accessed=4 * 1024 * 1024, transcendentals=0),
        name="local",
    )(w, x, own, hot, wide, mix)
    grad, sums = pl.pallas_call(
        adjoint_kernel,
        out_shape=(field, pltpu.VMEM((groups, 1, columns), f32)),
        in_specs=vmem(8),
        out_specs=tuple(vmem(2)),
        compiler_params=params(),
        name="adjoint",
    )(far, near, inner, halo, hot, ah, al, sums)
    sums = jnp.sum(lax.all_to_all(sums, "member", 0, 0), axis=0)
    sums = jnp.broadcast_to(sums[None], (tiles,) + sums.shape)
    sums = jnp.sum(lax.all_to_all(sums, "tile", 0, 0), axis=0)
    sums = jnp.sum(sums.reshape(2, columns // 2), axis=1) / cells
    return inc, grad[None], sums[1], sums[0]


def solution(mesh):
    placed = (
        P("member", None, None, "tile"),
        P("member", None, None, "tile"),
        P(None, None, "tile"),
        P(None, None, "tile"),
        P(),
    )
    return jax.shard_map(
        functools.partial(per_device, mesh.shape["tile"]),
        mesh=mesh,
        in_specs=placed,
        out_specs=(P("member", None, "tile"), P("member", None, None, "tile"), P(), P()),
        check_vma=False,
    )
```

```python
import functools

import jax
import jax.numpy as jnp
import numpy as np
from jax import lax
from jax.experimental import pallas as pl
from jax.experimental.pallas import tpu as pltpu
from jax.sharding import PartitionSpec as P

CLASSES = 4
PARTS = 2
VMEM_LIMIT = 48 * 1024 * 1024
f32, bf16 = jnp.float32, jnp.bfloat16


def vmem(count):
    return [pl.BlockSpec(memory_space=pltpu.VMEM)] * count


def params():
    return pltpu.CompilerParams(vmem_limit_bytes=VMEM_LIMIT)


def split(value):
    high = value.astype(bf16)
    low = (value - high.astype(f32)).astype(bf16)
    return high, low


def dot(a, b):
    return jnp.dot(a, b, preferred_element_type=f32)


def left_product(high, low, value):
    vhigh, vlow = split(value)
    width = value.shape[1]
    both = dot(high, jnp.concatenate([vhigh, vlow], axis=1))
    return both[:, :width] + both[:, width:] + dot(low, vhigh)


def class_product(value, hot_ref, band):
    width = value.shape[1]
    high, low = split(value)
    highs = jnp.concatenate([high * hot_ref[c] for c in range(CLASSES)], axis=1)
    lows = jnp.concatenate([low * hot_ref[c] for c in range(CLASSES)], axis=1)
    both = dot(highs, band)
    return both[:, :width] + both[:, width:] + dot(lows, band[:, :width])


def lane_is_low(shape, half):
    return lax.broadcasted_iota(jnp.int32, shape, len(shape) - 1) < half


def lane_swaps(shape, half):
    upper = lax.broadcasted_iota(jnp.int32, shape, len(shape) - 1) // half
    return (upper + lax.axis_index("tile")) % 2 == 0


def pack_halves(first, second, near_ref, far_ref, at):
    columns = first.shape[2]
    half = columns // 2
    turned = pltpu.roll(second.reshape(-1, columns), half, 1).reshape(second.shape)
    swap = lane_swaps(first.shape, half)
    near_ref[at] = jnp.where(swap, turned, first)
    far_ref[at] = jnp.where(swap, first, turned)


def unpack_halves(near, far):
    columns = near.shape[2]
    half = columns // 2
    swap = lane_swaps(near.shape, half)
    first = jnp.where(swap, near, far).reshape(-1, columns)
    second = pltpu.roll(jnp.where(swap, far, near).reshape(-1, columns), half, 1)
    return jnp.concatenate([first, second], axis=0)


def pack_kernel(x_hbm, far_ref, near_ref, x_ref, sems):
    half_levels = near_ref.shape[0]
    size = half_levels // PARTS
    copies = []
    for part in range(PARTS):
        for side in range(2):
            at = pl.ds(side * half_levels + part * size, size)
            copy = pltpu.make_async_copy(x_hbm.at[at], x_ref.at[at], sems.at[part, side])
            copy.start()
            copies.append(copy)
    for part in range(PARTS):
        copies[2 * part].wait()
        copies[2 * part + 1].wait()
        at = pl.ds(part * size, size)
        pack_halves(x_ref[at], x_ref[pl.ds(half_levels + part * size, size)], near_ref, far_ref, at)


def class_scale(c):
    return 1.0 + float(c)


def operators_kernel(
    classes_hbm, x_ref, weight_hbm, innovation_hbm,
    fh_ref, fl_ref, wide_ref, mix_ref, own_ref, halo_ref, hot_ref, y_ref, sum_ref, weight_ref, innovation_ref,
    classes, class_ref, class_rows_ref, sems,
):
    levels, lat, columns = x_ref.shape
    rows = levels * lat
    half = columns // 2
    share = weight_ref.shape[0]
    mine = pl.ds(lax.axis_index("member") * share, share)
    class_copy = pltpu.make_async_copy(classes_hbm, classes, sems.at[0])
    weight_copy = pltpu.make_async_copy(weight_hbm.at[mine], weight_ref, sems.at[1])
    innovation_copy = pltpu.make_async_copy(innovation_hbm.at[mine], innovation_ref, sems.at[2])
    class_copy.start()
    weight_copy.start()
    innovation_copy.start()
    d = lax.broadcasted_iota(jnp.int32, (columns, columns), 0)
    out = lax.broadcasted_iota(jnp.int32, (columns, columns), 1)
    for ref, place in ((own_ref, d), (halo_ref, jnp.where(d < half, d + columns, d - columns))):
        far = (place - out).astype(f32)
        inside = jnp.abs(far) <= half
        for c in range(CLASSES):
            sigma = half * class_scale(c) / 4.0
            e = np.arange(-half, half + 1, dtype=np.float32)
            norm = float(np.sqrt(np.sum(np.exp(-e * e / np.float32(sigma * sigma)), dtype=np.float32)))
            band = jnp.where(inside, jnp.exp(-far * far / (2.0 * sigma * sigma)) / norm, 0.0)
            at = pl.ds(c * columns, columns)
            ref[at, :columns], ref[at, columns:] = split(band)
    i = lax.broadcasted_iota(jnp.int32, (lat, rows), 0)
    j = lax.broadcasted_iota(jnp.int32, (lat, rows), 1) & (lat - 1)
    gap = (i - j).astype(f32)
    patterns = []
    for c in range(CLASSES):
        rho = lat * class_scale(c) / 8.0
        e = np.arange(-(lat - 1), lat, dtype=np.float32)
        norm = float(np.sqrt(np.sum(np.exp(-e * e / np.float32(rho * rho)), dtype=np.float32)))
        patterns.append(jnp.exp(-gap * gap / (2.0 * rho * rho)) / norm)
    ahead = lax.broadcasted_iota(jnp.int32, (levels, rows), 1) - lat * lax.broadcasted_iota(jnp.int32, (levels, rows), 0)
    spread = ((ahead >= 0) & (ahead < lat)).astype(f32).astype(bf16)
    k = lax.broadcasted_iota(jnp.int32, (levels, levels), 0)
    q = lax.broadcasted_iota(jnp.int32, (levels, levels), 1)
    spacing = (k - q).astype(f32)
    x = x_ref[...].reshape(rows, columns)
    sum_ref[...] = 0.5 * jnp.sum(x * x, axis=0, keepdims=True)
    class_copy.wait()
    for level in range(levels):
        class_ref[pl.ds(level, 1), :] = jnp.full((1, columns), classes[level].astype(f32), f32)
    class_lines = class_ref[...]
    class_rows = jnp.broadcast_to(class_lines[:, None, :], (levels, lat, columns)).reshape(rows, columns)
    class_rows_ref[...] = class_rows
    for c in range(CLASSES):
        hot_ref[c] = (class_rows == float(c)).astype(f32).astype(bf16)
    class_col = class_lines[:, :levels]
    class_row = jnp.sum(jnp.where(k == q, class_col, 0.0), axis=0, keepdims=True)
    scale_col = 1.0 + class_col
    scale_row = 1.0 + class_row
    vertical = jnp.exp(-spacing * spacing / (scale_col * scale_col + scale_row * scale_row))
    vh, vl = split(vertical)
    wide_ref[...] = dot(vh, spread) + dot(vl, spread)
    class_wide = dot(jnp.broadcast_to(class_row, (8, levels)).astype(bf16), spread)[:1]
    mix = jnp.zeros((lat, rows), f32)
    for c in range(CLASSES):
        mix = jnp.where(class_wide == float(c), patterns[c], mix)
    mix_ref[...] = mix
    for pair in range(levels // 2):
        both = []
        for level in (2 * pair, 2 * pair + 1):
            kind = class_rows_ref[pl.ds(level * lat, lat), :1]
            pattern = patterns[CLASSES - 1]
            for c in range(CLASSES - 1):
                pattern = jnp.where(kind == float(c), patterns[c], pattern)
            both.append(wide_ref[pl.ds(level, 1), :] * pattern)
        at = pl.ds(2 * pair * lat, 2 * lat)
        fh_ref[at, :], fl_ref[at, :] = split(jnp.concatenate(both, axis=0))
    y_ref[...] = class_product(left_product(fh_ref[...], fl_ref[...], x), hot_ref, own_ref[...])
    weight_copy.wait()
    innovation_copy.wait()


def forward_kernel(inverse, far_ref, near_ref, y_ref, fh_ref, flo_ref, halo_ref, hot_ref, m_ref, mine_ref, other_ref):
    levels, lat, columns = m_ref.shape
    halo = left_product(fh_ref[...], flo_ref[...], unpack_halves(near_ref[...], far_ref[...]))
    alpha = y_ref[...] + class_product(halo, hot_ref, halo_ref[...])
    term = m_ref[...].astype(f32) * alpha.reshape(levels, lat, columns) * inverse
    chips, share = mine_ref.shape[:2]
    term = term.reshape(chips, 2, share, lat, columns)
    even = lax.axis_index("member") % 2 == 0
    mine_ref[...] = jnp.where(even, term[:, 0], term[:, 1])
    other_ref[...] = jnp.where(even, term[:, 1], term[:, 0])


def add_kernel(mine_ref, sent_ref, out_ref):
    out_ref[...] = mine_ref[...] + sent_ref[1 - lax.axis_index("member") % 2]


def middle_kernel(got_ref, weight_ref, innovation_ref, sum_in, inc_ref, misfit_ref, sum_ref):
    inc = jnp.sum(got_ref[...], axis=0)
    weight, innovation = weight_ref[...], innovation_ref[...]
    inc_ref[...] = inc
    misfit_ref[...] = jnp.broadcast_to((weight * inc - innovation)[None], misfit_ref.shape)
    cost = 0.5 * weight * inc * inc - innovation * inc
    sum_ref[...] = sum_in[...] + jnp.sum(cost.reshape(-1, cost.shape[2]), axis=0, keepdims=True)


def weight_kernel(inverse, m_ref, both_ref, w_ref, far_ref, near_ref):
    levels, lat, columns = m_ref.shape
    misfit = jnp.stack([both_ref[0], both_ref[1]], axis=1)
    w = m_ref[...].astype(f32) * misfit.reshape(levels, lat, columns) * inverse
    w_ref[...] = w
    half_levels = near_ref.shape[0]
    pack_halves(w[:half_levels], w[half_levels:], near_ref, far_ref, slice(None))


def local_kernel(w_ref, x_ref, own_ref, hot_ref, wide_ref, mix_ref, inc_ref, out_ref, ah_ref, al_ref, inc_out):
    levels, lat, columns = w_ref.shape
    rows = levels * lat
    inc_out[...] = inc_ref[...]
    mix = mix_ref[...]
    for pair in range(levels // 2):
        both = [wide_ref[pl.ds(level, 1), :] * mix for level in (2 * pair, 2 * pair + 1)]
        at = pl.ds(2 * pair * lat, 2 * lat)
        ah_ref[at, :], al_ref[at, :] = split(jnp.concatenate(both, axis=0))
    filtered = class_product(w_ref[...].reshape(rows, columns), hot_ref, own_ref[...])
    part = left_product(ah_ref[...], al_ref[...], filtered)
    out_ref[...] = x_ref[...] + part.reshape(levels, lat, columns)


def adjoint_kernel(far_ref, near_ref, part_ref, halo_ref, hot_ref, ah_ref, al_ref, sum_in, grad_ref, sums_ref):
    levels, lat, columns = part_ref.shape
    half = columns // 2
    filtered = class_product(unpack_halves(near_ref[...], far_ref[...]), hot_ref, halo_ref[...])
    edge = left_product(ah_ref[...], al_ref[...], filtered)
    grad = part_ref[...] + edge.reshape(levels, lat, columns)
    grad_ref[...] = grad
    flat = grad.reshape(-1, columns)
    square = jnp.sum(flat * flat, axis=0, keepdims=True)
    cost = sum_in[...]
    row = jnp.where(lane_is_low(square.shape, half), square + pltpu.roll(square, half, 1), cost + pltpu.roll(cost, half, 1))
    sums_ref[...] = jnp.broadcast_to(row[None], sums_ref.shape)


def finish_kernel(cells, got_ref, square_ref, cost_ref):
    row = jnp.sum(got_ref[...], axis=0)
    low = lane_is_low(row.shape, row.shape[1] // 2)
    square_ref[...] = jnp.sum(jnp.where(low, row, 0.0), axis=1, keepdims=True) / cells
    cost_ref[...] = jnp.sum(jnp.where(low, 0.0, row), axis=1, keepdims=True) / cells


def per_device(tiles, control, members, obs_weight, innovation, scale_index):
    x = control[0]
    in_hbm = (x, obs_weight, innovation, scale_index)
    x_hbm, weight_hbm, innovation_hbm, classes = [pltpu.with_memory_space_constraint(v, pltpu.HBM) for v in in_hbm]
    member = members[0]
    levels, lat, columns = x.shape
    rows = levels * lat
    groups = lax.axis_size("member")
    share = levels // groups
    cells = float(groups * rows * columns * tiles)
    inverse = float(np.float32(1.0) / np.sqrt(np.float32(groups - 1)))
    half_pack = pltpu.VMEM((levels // 2, lat, columns), f32)
    field = pltpu.VMEM((levels, lat, columns), f32)
    part = pltpu.VMEM((share, lat, columns), f32)
    square = pltpu.VMEM((rows, rows), bf16)
    band = pltpu.VMEM((CLASSES * columns, 2 * columns), bf16)
    line = pltpu.VMEM((1, columns), f32)
    chips = [list(range(core, groups, 2)) for core in range(2)]
    cores = [[i, i + 1] for i in range(0, groups, 2)]
    near_pairs = [(i, i ^ 1) for i in range(tiles)]
    far_pairs = [(i, (((i - 1) % tiles ^ 1) + 1) % tiles) for i in range(tiles)]
    hbm = [pl.BlockSpec(memory_space=pltpu.HBM)]

    far, near, x_near = pl.pallas_call(
        pack_kernel,
        out_shape=(half_pack, half_pack, field),
        in_specs=hbm,
        out_specs=tuple(vmem(3)),
        scratch_shapes=[pltpu.SemaphoreType.DMA((PARTS, 2))],
        compiler_params=params(),
        name="pack_control",
    )(x_hbm)
    far = lax.ppermute(far, "tile", far_pairs)
    near = lax.ppermute(near, "tile", near_pairs)
    fh, fl, wide, mix, own, halo, hot, y, half_sum, weight_share, innovation_share = pl.pallas_call(
        operators_kernel,
        out_shape=(square, square, pltpu.VMEM((levels, rows), f32), pltpu.VMEM((lat, rows), f32), band, band, pltpu.VMEM((CLASSES, rows, columns), bf16), pltpu.VMEM((rows, columns), f32), line, part, part),
        in_specs=hbm + vmem(1) + hbm * 2,
        out_specs=tuple(vmem(11)),
        scratch_shapes=[
            pltpu.SMEM((levels,), jnp.int32),
            pltpu.VMEM((levels, columns), f32),
            pltpu.VMEM((rows, columns), f32),
            pltpu.SemaphoreType.DMA((3,)),
        ],
        compiler_params=params(),
        cost_estimate=pl.CostEstimate(flops=6 * rows * rows * columns, bytes_accessed=6 * 1024 * 1024, transcendentals=300000),
        name="operators",
    )(classes, x_near, weight_hbm, innovation_hbm)
    half_term = pltpu.VMEM((groups // 2, share, lat, columns), f32)
    mine, other = pl.pallas_call(
        functools.partial(forward_kernel, inverse),
        out_shape=(half_term, half_term),
        in_specs=vmem(8),
        out_specs=tuple(vmem(2)),
        compiler_params=params(),
        name="forward",
    )(far, near, y, fh, fl, halo, hot, member)
    sent = lax.all_gather(other, "member", axis_index_groups=cores)
    both = pl.pallas_call(add_kernel, out_shape=half_term, in_specs=vmem(2), out_specs=vmem(1)[0], compiler_params=params(), name="add_cores")(mine, sent)
    got = lax.all_to_all(both, "member", 0, 0, axis_index_groups=chips)
    inc, misfit_share, sums = pl.pallas_call(
        middle_kernel,
        out_shape=(part, pltpu.VMEM((groups // 2, share, lat, columns), f32), line),
        in_specs=vmem(4),
        out_specs=tuple(vmem(3)),
        compiler_params=params(),
        name="middle",
    )(got, weight_share, innovation_share, half_sum)
    misfit_mine = lax.all_to_all(misfit_share, "member", 0, 0, axis_index_groups=chips)
    misfit = lax.all_gather(misfit_mine, "member", axis_index_groups=cores)
    w, far, near = pl.pallas_call(
        functools.partial(weight_kernel, inverse),
        out_shape=(field, half_pack, half_pack),
        in_specs=vmem(2),
        out_specs=tuple(vmem(3)),
        compiler_params=params(),
        name="weighted",
    )(member, misfit)
    far = lax.ppermute(far, "tile", far_pairs)
    near = lax.ppermute(near, "tile", near_pairs)
    inner, ah, al, inc = pl.pallas_call(
        local_kernel,
        out_shape=(field, square, square, jax.ShapeDtypeStruct(inc.shape, f32)),
        in_specs=vmem(7),
        out_specs=tuple(vmem(4)),
        compiler_params=params(),
        cost_estimate=pl.CostEstimate(flops=8 * rows * rows * columns, bytes_accessed=4 * 1024 * 1024, transcendentals=0),
        name="local",
    )(w, x, own, hot, wide, mix, inc)
    grad, sums = pl.pallas_call(
        adjoint_kernel,
        out_shape=(field, pltpu.VMEM((groups, 1, columns), f32)),
        in_specs=vmem(8),
        out_specs=tuple(vmem(2)),
        compiler_params=params(),
        name="adjoint",
    )(far, near, inner, halo, hot, ah, al, sums)
    sums = jnp.sum(lax.all_to_all(sums, "member", 0, 0), axis=0)
    sums = jnp.broadcast_to(sums[None], (tiles,) + sums.shape)
    one = jax.ShapeDtypeStruct((1, 1), f32)
    square_mean, cost = pl.pallas_call(
        functools.partial(finish_kernel, cells),
        out_shape=(one, one),
        in_specs=vmem(1),
        out_specs=tuple(vmem(2)),
        compiler_params=params(),
        name="finish",
    )(lax.all_to_all(sums, "tile", 0, 0))
    return inc, grad[None], cost.reshape(()), square_mean.reshape(())


def solution(mesh):
    placed = (
        P("member", None, None, "tile"),
        P("member", None, None, "tile"),
        P(None, None, "tile"),
        P(None, None, "tile"),
        P(),
    )
    return jax.shard_map(
        functools.partial(per_device, mesh.shape["tile"]),
        mesh=mesh,
        in_specs=placed,
        out_specs=(P("member", None, "tile"), P("member", None, None, "tile"), P(), P()),
        check_vma=False,
    )
```

```python
import functools

import jax
import jax.numpy as jnp
import numpy as np
from jax import lax
from jax.experimental import pallas as pl
from jax.experimental.pallas import tpu as pltpu
from jax.sharding import PartitionSpec as P

CLASSES = 4
PARTS = 2
VMEM_LIMIT = 48 * 1024 * 1024
f32, bf16 = jnp.float32, jnp.bfloat16


def vmem(count):
    return [pl.BlockSpec(memory_space=pltpu.VMEM)] * count


def params():
    return pltpu.CompilerParams(vmem_limit_bytes=VMEM_LIMIT)


def split(value):
    high = value.astype(bf16)
    low = (value - high.astype(f32)).astype(bf16)
    return high, low


def dot(a, b):
    return jnp.dot(a, b, preferred_element_type=f32)


def left_product(high, low, value):
    vhigh, vlow = split(value)
    width = value.shape[1]
    both = dot(high, jnp.concatenate([vhigh, vlow], axis=1))
    return both[:, :width] + both[:, width:] + dot(low, vhigh)


def class_product(value, hot_ref, band):
    width = value.shape[1]
    high, low = split(value)
    highs = jnp.concatenate([high * hot_ref[c] for c in range(CLASSES)], axis=1)
    lows = jnp.concatenate([low * hot_ref[c] for c in range(CLASSES)], axis=1)
    both = dot(highs, band)
    return both[:, :width] + both[:, width:] + dot(lows, band[:, :width])


def lane_is_low(shape, half):
    return lax.broadcasted_iota(jnp.int32, shape, len(shape) - 1) < half


def lane_swaps(shape, half):
    upper = lax.broadcasted_iota(jnp.int32, shape, len(shape) - 1) // half
    return (upper + lax.axis_index("tile")) % 2 == 0


def pack_halves(first, second, near_ref, far_ref, at):
    columns = first.shape[2]
    half = columns // 2
    turned = pltpu.roll(second.reshape(-1, columns), half, 1).reshape(second.shape)
    swap = lane_swaps(first.shape, half)
    near_ref[at] = jnp.where(swap, turned, first)
    far_ref[at] = jnp.where(swap, first, turned)


def unpack_halves(near, far):
    columns = near.shape[2]
    half = columns // 2
    swap = lane_swaps(near.shape, half)
    first = jnp.where(swap, near, far).reshape(-1, columns)
    second = pltpu.roll(jnp.where(swap, far, near).reshape(-1, columns), half, 1)
    return jnp.concatenate([first, second], axis=0)


def pack_kernel(x_hbm, far_ref, near_ref, x_ref, sems):
    half_levels = near_ref.shape[0]
    size = half_levels // PARTS
    copies = []
    for part in range(PARTS):
        for side in range(2):
            at = pl.ds(side * half_levels + part * size, size)
            copy = pltpu.make_async_copy(x_hbm.at[at], x_ref.at[at], sems.at[part, side])
            copy.start()
            copies.append(copy)
    for part in range(PARTS):
        copies[2 * part].wait()
        copies[2 * part + 1].wait()
        at = pl.ds(part * size, size)
        pack_halves(x_ref[at], x_ref[pl.ds(half_levels + part * size, size)], near_ref, far_ref, at)


def class_scale(c):
    return 1.0 + float(c)


def operators_kernel(
    classes_hbm, x_ref, weight_hbm, innovation_hbm,
    fh_ref, fl_ref, wide_ref, mix_ref, own_ref, halo_ref, hot_ref, y_ref, sum_ref, weight_ref, innovation_ref,
    classes, class_ref, class_rows_ref, sems,
):
    levels, lat, columns = x_ref.shape
    rows = levels * lat
    half = columns // 2
    share = weight_ref.shape[0]
    mine = pl.ds(lax.axis_index("member") * share, share)
    class_copy = pltpu.make_async_copy(classes_hbm, classes, sems.at[0])
    weight_copy = pltpu.make_async_copy(weight_hbm.at[mine], weight_ref, sems.at[1])
    innovation_copy = pltpu.make_async_copy(innovation_hbm.at[mine], innovation_ref, sems.at[2])
    class_copy.start()
    weight_copy.start()
    innovation_copy.start()
    d = lax.broadcasted_iota(jnp.int32, (columns, columns), 0)
    out = lax.broadcasted_iota(jnp.int32, (columns, columns), 1)
    for ref, place in ((own_ref, d), (halo_ref, jnp.where(d < half, d + columns, d - columns))):
        far = (place - out).astype(f32)
        inside = jnp.abs(far) <= half
        for c in range(CLASSES):
            sigma = half * class_scale(c) / 4.0
            e = np.arange(-half, half + 1, dtype=np.float32)
            norm = float(np.sqrt(np.sum(np.exp(-e * e / np.float32(sigma * sigma)), dtype=np.float32)))
            band = jnp.where(inside, jnp.exp(-far * far / (2.0 * sigma * sigma)) / norm, 0.0)
            at = pl.ds(c * columns, columns)
            ref[at, :columns], ref[at, columns:] = split(band)
    i = lax.broadcasted_iota(jnp.int32, (lat, rows), 0)
    j = lax.broadcasted_iota(jnp.int32, (lat, rows), 1) & (lat - 1)
    gap = (i - j).astype(f32)
    patterns = []
    for c in range(CLASSES):
        rho = lat * class_scale(c) / 8.0
        e = np.arange(-(lat - 1), lat, dtype=np.float32)
        norm = float(np.sqrt(np.sum(np.exp(-e * e / np.float32(rho * rho)), dtype=np.float32)))
        patterns.append(jnp.exp(-gap * gap / (2.0 * rho * rho)) / norm)
    ahead = lax.broadcasted_iota(jnp.int32, (levels, rows), 1) - lat * lax.broadcasted_iota(jnp.int32, (levels, rows), 0)
    spread = ((ahead >= 0) & (ahead < lat)).astype(f32).astype(bf16)
    k = lax.broadcasted_iota(jnp.int32, (levels, levels), 0)
    q = lax.broadcasted_iota(jnp.int32, (levels, levels), 1)
    spacing = (k - q).astype(f32)
    x = x_ref[...].reshape(rows, columns)
    sum_ref[...] = 0.5 * jnp.sum(x * x, axis=0, keepdims=True)
    class_copy.wait()
    for level in range(levels):
        class_ref[pl.ds(level, 1), :] = jnp.full((1, columns), classes[level].astype(f32), f32)
    class_lines = class_ref[...]
    class_rows = jnp.broadcast_to(class_lines[:, None, :], (levels, lat, columns)).reshape(rows, columns)
    class_rows_ref[...] = class_rows
    for c in range(CLASSES):
        hot_ref[c] = (class_rows == float(c)).astype(f32).astype(bf16)
    class_col = class_lines[:, :levels]
    class_row = jnp.sum(jnp.where(k == q, class_col, 0.0), axis=0, keepdims=True)
    scale_col = 1.0 + class_col
    scale_row = 1.0 + class_row
    vertical = jnp.exp(-spacing * spacing / (scale_col * scale_col + scale_row * scale_row))
    vh, vl = split(vertical)
    wide_ref[...] = dot(vh, spread) + dot(vl, spread)
    class_wide = dot(jnp.broadcast_to(class_row, (8, levels)).astype(bf16), spread)[:1]
    mix = jnp.zeros((lat, rows), f32)
    for c in range(CLASSES):
        mix = jnp.where(class_wide == float(c), patterns[c], mix)
    mix_ref[...] = mix
    for pair in range(levels // 2):
        both = []
        for level in (2 * pair, 2 * pair + 1):
            kind = class_rows_ref[pl.ds(level * lat, lat), :1]
            pattern = patterns[CLASSES - 1]
            for c in range(CLASSES - 1):
                pattern = jnp.where(kind == float(c), patterns[c], pattern)
            both.append(wide_ref[pl.ds(level, 1), :] * pattern)
        at = pl.ds(2 * pair * lat, 2 * lat)
        fh_ref[at, :], fl_ref[at, :] = split(jnp.concatenate(both, axis=0))
    y_ref[...] = class_product(left_product(fh_ref[...], fl_ref[...], x), hot_ref, own_ref[...])
    weight_copy.wait()
    innovation_copy.wait()


def forward_kernel(inverse, far_ref, near_ref, y_ref, fh_ref, flo_ref, halo_ref, hot_ref, m_ref, mine_ref, other_ref):
    levels, lat, columns = m_ref.shape
    halo = left_product(fh_ref[...], flo_ref[...], unpack_halves(near_ref[...], far_ref[...]))
    alpha = y_ref[...] + class_product(halo, hot_ref, halo_ref[...])
    term = m_ref[...].astype(f32) * alpha.reshape(levels, lat, columns) * inverse
    chips, share = mine_ref.shape[:2]
    term = term.reshape(chips, 2, share, lat, columns)
    even = lax.axis_index("member") % 2 == 0
    mine_ref[...] = jnp.where(even, term[:, 0], term[:, 1])
    other_ref[...] = jnp.where(even, term[:, 1], term[:, 0])


def add_kernel(mine_ref, sent_ref, out_ref):
    out_ref[...] = mine_ref[...] + sent_ref[1 - lax.axis_index("member") % 2]


def middle_kernel(got_ref, weight_ref, innovation_ref, sum_in, inc_ref, misfit_ref, sum_ref):
    inc = jnp.sum(got_ref[...], axis=0)
    weight, innovation = weight_ref[...], innovation_ref[...]
    inc_ref[...] = inc
    misfit_ref[...] = jnp.broadcast_to((weight * inc - innovation)[None], misfit_ref.shape)
    cost = 0.5 * weight * inc * inc - innovation * inc
    sum_ref[...] = sum_in[...] + jnp.sum(cost.reshape(-1, cost.shape[2]), axis=0, keepdims=True)


def weight_kernel(inverse, m_ref, both_ref, w_ref, far_ref, near_ref):
    levels, lat, columns = m_ref.shape
    misfit = jnp.stack([both_ref[0], both_ref[1]], axis=1)
    w = m_ref[...].astype(f32) * misfit.reshape(levels, lat, columns) * inverse
    w_ref[...] = w
    half_levels = near_ref.shape[0]
    pack_halves(w[:half_levels], w[half_levels:], near_ref, far_ref, slice(None))


def local_kernel(w_ref, x_ref, own_ref, hot_ref, wide_ref, mix_ref, out_ref, ah_ref, al_ref):
    levels, lat, columns = w_ref.shape
    rows = levels * lat
    mix = mix_ref[...]
    for pair in range(levels // 2):
        both = [wide_ref[pl.ds(level, 1), :] * mix for level in (2 * pair, 2 * pair + 1)]
        at = pl.ds(2 * pair * lat, 2 * lat)
        ah_ref[at, :], al_ref[at, :] = split(jnp.concatenate(both, axis=0))
    filtered = class_product(w_ref[...].reshape(rows, columns), hot_ref, own_ref[...])
    part = left_product(ah_ref[...], al_ref[...], filtered)
    out_ref[...] = x_ref[...] + part.reshape(levels, lat, columns)


def adjoint_kernel(far_ref, near_ref, part_ref, halo_ref, hot_ref, ah_ref, al_ref, sum_in, grad_ref, sums_ref):
    levels, lat, columns = part_ref.shape
    half = columns // 2
    filtered = class_product(unpack_halves(near_ref[...], far_ref[...]), hot_ref, halo_ref[...])
    edge = left_product(ah_ref[...], al_ref[...], filtered)
    grad = part_ref[...] + edge.reshape(levels, lat, columns)
    grad_ref[...] = grad
    flat = grad.reshape(-1, columns)
    square = jnp.sum(flat * flat, axis=0, keepdims=True)
    cost = sum_in[...]
    row = jnp.where(lane_is_low(square.shape, half), square + pltpu.roll(square, half, 1), cost + pltpu.roll(cost, half, 1))
    sums_ref[...] = jnp.broadcast_to(row[None], sums_ref.shape)


def finish_kernel(cells, got_ref, grad_ref, inc_ref, square_hbm, cost_hbm, grad_hbm, inc_hbm, square_ref, cost_ref, sems):
    copies = [
        pltpu.make_async_copy(grad_ref, grad_hbm, sems.at[0]),
        pltpu.make_async_copy(square_ref, square_hbm, sems.at[1]),
        pltpu.make_async_copy(cost_ref, cost_hbm, sems.at[2]),
        pltpu.make_async_copy(inc_ref, inc_hbm, sems.at[3]),
    ]
    copies[0].start()
    copies[3].start()
    row = jnp.sum(got_ref[...], axis=0)
    low = lane_is_low(row.shape, row.shape[1] // 2)
    square_ref[...] = jnp.sum(jnp.where(low, row, 0.0), axis=1, keepdims=True) / cells
    cost_ref[...] = jnp.sum(jnp.where(low, 0.0, row), axis=1, keepdims=True) / cells
    copies[1].start()
    copies[2].start()
    for copy in copies:
        copy.wait()


def per_device(tiles, control, members, obs_weight, innovation, scale_index):
    x = control[0]
    in_hbm = (x, obs_weight, innovation, scale_index)
    x_hbm, weight_hbm, innovation_hbm, classes = [pltpu.with_memory_space_constraint(v, pltpu.HBM) for v in in_hbm]
    member = members[0]
    levels, lat, columns = x.shape
    rows = levels * lat
    groups = lax.axis_size("member")
    share = levels // groups
    cells = float(groups * rows * columns * tiles)
    inverse = float(np.float32(1.0) / np.sqrt(np.float32(groups - 1)))
    half_pack = pltpu.VMEM((levels // 2, lat, columns), f32)
    field = pltpu.VMEM((levels, lat, columns), f32)
    part = pltpu.VMEM((share, lat, columns), f32)
    square = pltpu.VMEM((rows, rows), bf16)
    band = pltpu.VMEM((CLASSES * columns, 2 * columns), bf16)
    line = pltpu.VMEM((1, columns), f32)
    chips = [list(range(core, groups, 2)) for core in range(2)]
    cores = [[i, i + 1] for i in range(0, groups, 2)]
    near_pairs = [(i, i ^ 1) for i in range(tiles)]
    far_pairs = [(i, (((i - 1) % tiles ^ 1) + 1) % tiles) for i in range(tiles)]
    hbm = [pl.BlockSpec(memory_space=pltpu.HBM)]

    far, near, x_near = pl.pallas_call(
        pack_kernel,
        out_shape=(half_pack, half_pack, field),
        in_specs=hbm,
        out_specs=tuple(vmem(3)),
        scratch_shapes=[pltpu.SemaphoreType.DMA((PARTS, 2))],
        compiler_params=params(),
        name="pack_control",
    )(x_hbm)
    far = lax.ppermute(far, "tile", far_pairs)
    near = lax.ppermute(near, "tile", near_pairs)
    fh, fl, wide, mix, own, halo, hot, y, half_sum, weight_share, innovation_share = pl.pallas_call(
        operators_kernel,
        out_shape=(square, square, pltpu.VMEM((levels, rows), f32), pltpu.VMEM((lat, rows), f32), band, band, pltpu.VMEM((CLASSES, rows, columns), bf16), pltpu.VMEM((rows, columns), f32), line, part, part),
        in_specs=hbm + vmem(1) + hbm * 2,
        out_specs=tuple(vmem(11)),
        scratch_shapes=[
            pltpu.SMEM((levels,), jnp.int32),
            pltpu.VMEM((levels, columns), f32),
            pltpu.VMEM((rows, columns), f32),
            pltpu.SemaphoreType.DMA((3,)),
        ],
        compiler_params=params(),
        cost_estimate=pl.CostEstimate(flops=6 * rows * rows * columns, bytes_accessed=6 * 1024 * 1024, transcendentals=300000),
        name="operators",
    )(classes, x_near, weight_hbm, innovation_hbm)
    half_term = pltpu.VMEM((groups // 2, share, lat, columns), f32)
    mine, other = pl.pallas_call(
        functools.partial(forward_kernel, inverse),
        out_shape=(half_term, half_term),
        in_specs=vmem(8),
        out_specs=tuple(vmem(2)),
        compiler_params=params(),
        name="forward",
    )(far, near, y, fh, fl, halo, hot, member)
    sent = lax.all_gather(other, "member", axis_index_groups=cores)
    both = pl.pallas_call(add_kernel, out_shape=half_term, in_specs=vmem(2), out_specs=vmem(1)[0], compiler_params=params(), name="add_cores")(mine, sent)
    got = lax.all_to_all(both, "member", 0, 0, axis_index_groups=chips)
    inc, misfit_share, sums = pl.pallas_call(
        middle_kernel,
        out_shape=(part, pltpu.VMEM((groups // 2, share, lat, columns), f32), line),
        in_specs=vmem(4),
        out_specs=tuple(vmem(3)),
        compiler_params=params(),
        name="middle",
    )(got, weight_share, innovation_share, half_sum)
    misfit_mine = lax.all_to_all(misfit_share, "member", 0, 0, axis_index_groups=chips)
    misfit = lax.all_gather(misfit_mine, "member", axis_index_groups=cores)
    w, far, near = pl.pallas_call(
        functools.partial(weight_kernel, inverse),
        out_shape=(field, half_pack, half_pack),
        in_specs=vmem(2),
        out_specs=tuple(vmem(3)),
        compiler_params=params(),
        name="weighted",
    )(member, misfit)
    far = lax.ppermute(far, "tile", far_pairs)
    near = lax.ppermute(near, "tile", near_pairs)
    inner, ah, al = pl.pallas_call(
        local_kernel,
        out_shape=(field, square, square),
        in_specs=vmem(6),
        out_specs=tuple(vmem(3)),
        compiler_params=params(),
        cost_estimate=pl.CostEstimate(flops=8 * rows * rows * columns, bytes_accessed=4 * 1024 * 1024, transcendentals=0),
        name="local",
    )(w, x, own, hot, wide, mix)
    grad, sums = pl.pallas_call(
        adjoint_kernel,
        out_shape=(field, pltpu.VMEM((groups, 1, columns), f32)),
        in_specs=vmem(8),
        out_specs=tuple(vmem(2)),
        compiler_params=params(),
        name="adjoint",
    )(far, near, inner, halo, hot, ah, al, sums)
    sums = jnp.sum(lax.all_to_all(sums, "member", 0, 0), axis=0)
    sums = jnp.broadcast_to(sums[None], (tiles,) + sums.shape)
    one = pltpu.HBM((1, 1), f32)
    square_mean, cost, grad, inc = pl.pallas_call(
        functools.partial(finish_kernel, cells),
        out_shape=(one, one, pltpu.HBM(grad.shape, f32), pltpu.HBM(inc.shape, f32)),
        in_specs=vmem(3),
        out_specs=tuple(hbm * 4),
        scratch_shapes=[pltpu.VMEM((1, 1), f32), pltpu.VMEM((1, 1), f32), pltpu.SemaphoreType.DMA((4,))],
        compiler_params=params(),
        name="finish",
    )(lax.all_to_all(sums, "tile", 0, 0), grad, inc)
    return inc, grad[None], cost.reshape(()), square_mean.reshape(())


def solution(mesh):
    placed = (
        P("member", None, None, "tile"),
        P("member", None, None, "tile"),
        P(None, None, "tile"),
        P(None, None, "tile"),
        P(),
    )
    return jax.shard_map(
        functools.partial(per_device, mesh.shape["tile"]),
        mesh=mesh,
        in_specs=placed,
        out_specs=(P("member", None, "tile"), P("member", None, None, "tile"), P(), P()),
        check_vma=False,
    )
```

```python
import functools

import jax
import jax.numpy as jnp
import numpy as np
from jax import lax
from jax.experimental import pallas as pl
from jax.experimental.pallas import tpu as pltpu
from jax.sharding import PartitionSpec as P

CLASSES = 4
PARTS = 2
VMEM_LIMIT = 48 * 1024 * 1024
f32, bf16 = jnp.float32, jnp.bfloat16


def vmem(count):
    return [pl.BlockSpec(memory_space=pltpu.VMEM)] * count


def params():
    return pltpu.CompilerParams(vmem_limit_bytes=VMEM_LIMIT)


def split(value):
    high = value.astype(bf16)
    low = (value - high.astype(f32)).astype(bf16)
    return high, low


def dot(a, b):
    return jnp.dot(a, b, preferred_element_type=f32)


def left_product(high, low, value):
    vhigh, vlow = split(value)
    width = value.shape[1]
    both = dot(high, jnp.concatenate([vhigh, vlow], axis=1))
    return both[:, :width] + both[:, width:] + dot(low, vhigh)


def class_product(value, hot_ref, band):
    width = value.shape[1]
    high, low = split(value)
    highs = jnp.concatenate([high * hot_ref[c] for c in range(CLASSES)], axis=1)
    lows = jnp.concatenate([low * hot_ref[c] for c in range(CLASSES)], axis=1)
    both = dot(highs, band)
    return both[:, :width] + both[:, width:] + dot(lows, band[:, :width])


def lane_is_low(shape, half):
    return lax.broadcasted_iota(jnp.int32, shape, len(shape) - 1) < half


def lane_swaps(shape, half):
    upper = lax.broadcasted_iota(jnp.int32, shape, len(shape) - 1) // half
    return (upper + lax.axis_index("tile")) % 2 == 0


def pack_halves(first, second, near_ref, far_ref, at):
    columns = first.shape[2]
    half = columns // 2
    turned = pltpu.roll(second.reshape(-1, columns), half, 1).reshape(second.shape)
    swap = lane_swaps(first.shape, half)
    near_ref[at] = jnp.where(swap, turned, first)
    far_ref[at] = jnp.where(swap, first, turned)


def unpack_halves(near, far):
    columns = near.shape[2]
    half = columns // 2
    swap = lane_swaps(near.shape, half)
    first = jnp.where(swap, near, far).reshape(-1, columns)
    second = pltpu.roll(jnp.where(swap, far, near).reshape(-1, columns), half, 1)
    return jnp.concatenate([first, second], axis=0)


def pack_kernel(x_hbm, far_ref, near_ref, x_ref, sems):
    half_levels = near_ref.shape[0]
    size = half_levels // PARTS
    copies = []
    for part in range(PARTS):
        for side in range(2):
            at = pl.ds(side * half_levels + part * size, size)
            copy = pltpu.make_async_copy(x_hbm.at[at], x_ref.at[at], sems.at[part, side])
            copy.start()
            copies.append(copy)
    for part in range(PARTS):
        copies[2 * part].wait()
        copies[2 * part + 1].wait()
        at = pl.ds(part * size, size)
        pack_halves(x_ref[at], x_ref[pl.ds(half_levels + part * size, size)], near_ref, far_ref, at)


def class_scale(c):
    return 1.0 + float(c)


def operators_kernel(
    inverse,
    classes_hbm, x_ref, m_ref, weight_hbm, innovation_hbm,
    fh_ref, fl_ref, wide_ref, mix_ref, own_ref, halo_ref, hot_ref, y_ref, scaled_ref, sum_ref, weight_ref, innovation_ref,
    classes, class_ref, class_rows_ref, sems,
):
    levels, lat, columns = x_ref.shape
    rows = levels * lat
    half = columns // 2
    share = weight_ref.shape[0]
    mine = pl.ds(lax.axis_index("member") * share, share)
    class_copy = pltpu.make_async_copy(classes_hbm, classes, sems.at[0])
    weight_copy = pltpu.make_async_copy(weight_hbm.at[mine], weight_ref, sems.at[1])
    innovation_copy = pltpu.make_async_copy(innovation_hbm.at[mine], innovation_ref, sems.at[2])
    class_copy.start()
    weight_copy.start()
    innovation_copy.start()
    d = lax.broadcasted_iota(jnp.int32, (columns, columns), 0)
    out = lax.broadcasted_iota(jnp.int32, (columns, columns), 1)
    for ref, place in ((own_ref, d), (halo_ref, jnp.where(d < half, d + columns, d - columns))):
        far = (place - out).astype(f32)
        inside = jnp.abs(far) <= half
        for c in range(CLASSES):
            sigma = half * class_scale(c) / 4.0
            e = np.arange(-half, half + 1, dtype=np.float32)
            norm = float(np.sqrt(np.sum(np.exp(-e * e / np.float32(sigma * sigma)), dtype=np.float32)))
            band = jnp.where(inside, jnp.exp(-far * far / (2.0 * sigma * sigma)) / norm, 0.0)
            at = pl.ds(c * columns, columns)
            ref[at, :columns], ref[at, columns:] = split(band)
    i = lax.broadcasted_iota(jnp.int32, (lat, rows), 0)
    j = lax.broadcasted_iota(jnp.int32, (lat, rows), 1) & (lat - 1)
    gap = (i - j).astype(f32)
    patterns = []
    for c in range(CLASSES):
        rho = lat * class_scale(c) / 8.0
        e = np.arange(-(lat - 1), lat, dtype=np.float32)
        norm = float(np.sqrt(np.sum(np.exp(-e * e / np.float32(rho * rho)), dtype=np.float32)))
        patterns.append(jnp.exp(-gap * gap / (2.0 * rho * rho)) / norm)
    ahead = lax.broadcasted_iota(jnp.int32, (levels, rows), 1) - lat * lax.broadcasted_iota(jnp.int32, (levels, rows), 0)
    spread = ((ahead >= 0) & (ahead < lat)).astype(f32).astype(bf16)
    k = lax.broadcasted_iota(jnp.int32, (levels, levels), 0)
    q = lax.broadcasted_iota(jnp.int32, (levels, levels), 1)
    spacing = (k - q).astype(f32)
    x = x_ref[...].reshape(rows, columns)
    sum_ref[...] = 0.5 * jnp.sum(x * x, axis=0, keepdims=True)
    class_copy.wait()
    for level in range(levels):
        class_ref[pl.ds(level, 1), :] = jnp.full((1, columns), classes[level].astype(f32), f32)
    class_lines = class_ref[...]
    class_rows = jnp.broadcast_to(class_lines[:, None, :], (levels, lat, columns)).reshape(rows, columns)
    class_rows_ref[...] = class_rows
    for c in range(CLASSES):
        hot_ref[c] = (class_rows == float(c)).astype(f32).astype(bf16)
    class_col = class_lines[:, :levels]
    class_row = jnp.sum(jnp.where(k == q, class_col, 0.0), axis=0, keepdims=True)
    scale_col = 1.0 + class_col
    scale_row = 1.0 + class_row
    vertical = jnp.exp(-spacing * spacing / (scale_col * scale_col + scale_row * scale_row))
    vh, vl = split(vertical)
    wide_ref[...] = dot(vh, spread) + dot(vl, spread)
    class_wide = dot(jnp.broadcast_to(class_row, (8, levels)).astype(bf16), spread)[:1]
    mix = jnp.zeros((lat, rows), f32)
    for c in range(CLASSES):
        mix = jnp.where(class_wide == float(c), patterns[c], mix)
    mix_ref[...] = mix
    for pair in range(levels // 2):
        both = []
        for level in (2 * pair, 2 * pair + 1):
            kind = class_rows_ref[pl.ds(level * lat, lat), :1]
            pattern = patterns[CLASSES - 1]
            for c in range(CLASSES - 1):
                pattern = jnp.where(kind == float(c), patterns[c], pattern)
            both.append(wide_ref[pl.ds(level, 1), :] * pattern)
        at = pl.ds(2 * pair * lat, 2 * lat)
        fh_ref[at, :], fl_ref[at, :] = split(jnp.concatenate(both, axis=0))
    scaled = m_ref[...].astype(f32) * inverse
    scaled_ref[...] = scaled
    y_ref[...] = scaled.reshape(rows, columns) * class_product(left_product(fh_ref[...], fl_ref[...], x), hot_ref, own_ref[...])
    weight_copy.wait()
    innovation_copy.wait()


def forward_kernel(far_ref, near_ref, y_ref, fh_ref, flo_ref, halo_ref, hot_ref, m_ref, mine_ref, other_ref):
    levels, lat, columns = m_ref.shape
    halo = left_product(fh_ref[...], flo_ref[...], unpack_halves(near_ref[...], far_ref[...]))
    edge = class_product(halo, hot_ref, halo_ref[...])
    term = y_ref[...].reshape(levels, lat, columns) + m_ref[...] * edge.reshape(levels, lat, columns)
    chips, share = mine_ref.shape[:2]
    term = term.reshape(chips, 2, share, lat, columns)
    even = lax.axis_index("member") % 2 == 0
    mine_ref[...] = jnp.where(even, term[:, 0], term[:, 1])
    other_ref[...] = jnp.where(even, term[:, 1], term[:, 0])


def add_kernel(mine_ref, sent_ref, out_ref):
    out_ref[...] = mine_ref[...] + sent_ref[1 - lax.axis_index("member") % 2]


def middle_kernel(got_ref, weight_ref, innovation_ref, sum_in, inc_ref, misfit_ref, sum_ref):
    inc = jnp.sum(got_ref[...], axis=0)
    weight, innovation = weight_ref[...], innovation_ref[...]
    inc_ref[...] = inc
    misfit_ref[...] = jnp.broadcast_to((weight * inc - innovation)[None], misfit_ref.shape)
    cost = 0.5 * weight * inc * inc - innovation * inc
    sum_ref[...] = sum_in[...] + jnp.sum(cost.reshape(-1, cost.shape[2]), axis=0, keepdims=True)


def weight_kernel(m_ref, both_ref, w_ref, far_ref, near_ref):
    levels, lat, columns = m_ref.shape
    misfit = jnp.stack([both_ref[0], both_ref[1]], axis=1)
    w = m_ref[...] * misfit.reshape(levels, lat, columns)
    w_ref[...] = w
    half_levels = near_ref.shape[0]
    pack_halves(w[:half_levels], w[half_levels:], near_ref, far_ref, slice(None))


def local_kernel(w_ref, x_ref, own_ref, hot_ref, wide_ref, mix_ref, out_ref, ah_ref, al_ref):
    levels, lat, columns = w_ref.shape
    rows = levels * lat
    mix = mix_ref[...]
    for pair in range(levels // 2):
        both = [wide_ref[pl.ds(level, 1), :] * mix for level in (2 * pair, 2 * pair + 1)]
        at = pl.ds(2 * pair * lat, 2 * lat)
        ah_ref[at, :], al_ref[at, :] = split(jnp.concatenate(both, axis=0))
    filtered = class_product(w_ref[...].reshape(rows, columns), hot_ref, own_ref[...])
    part = left_product(ah_ref[...], al_ref[...], filtered)
    out_ref[...] = x_ref[...] + part.reshape(levels, lat, columns)


def adjoint_kernel(far_ref, near_ref, part_ref, halo_ref, hot_ref, ah_ref, al_ref, sum_in, grad_ref, sums_ref):
    levels, lat, columns = part_ref.shape
    half = columns // 2
    filtered = class_product(unpack_halves(near_ref[...], far_ref[...]), hot_ref, halo_ref[...])
    edge = left_product(ah_ref[...], al_ref[...], filtered)
    grad = part_ref[...] + edge.reshape(levels, lat, columns)
    grad_ref[...] = grad
    flat = grad.reshape(-1, columns)
    square = jnp.sum(flat * flat, axis=0, keepdims=True)
    cost = sum_in[...]
    row = jnp.where(lane_is_low(square.shape, half), square + pltpu.roll(square, half, 1), cost + pltpu.roll(cost, half, 1))
    sums_ref[...] = jnp.broadcast_to(row[None], sums_ref.shape)


def finish_kernel(cells, got_ref, grad_ref, inc_ref, square_hbm, cost_hbm, grad_hbm, inc_hbm, square_ref, cost_ref, sems):
    copies = [
        pltpu.make_async_copy(grad_ref, grad_hbm, sems.at[0]),
        pltpu.make_async_copy(square_ref, square_hbm, sems.at[1]),
        pltpu.make_async_copy(cost_ref, cost_hbm, sems.at[2]),
        pltpu.make_async_copy(inc_ref, inc_hbm, sems.at[3]),
    ]
    copies[0].start()
    copies[3].start()
    row = jnp.sum(got_ref[...], axis=0)
    low = lane_is_low(row.shape, row.shape[1] // 2)
    square_ref[...] = jnp.sum(jnp.where(low, row, 0.0), axis=1, keepdims=True) / cells
    cost_ref[...] = jnp.sum(jnp.where(low, 0.0, row), axis=1, keepdims=True) / cells
    copies[1].start()
    copies[2].start()
    for copy in copies:
        copy.wait()


def per_device(tiles, control, members, obs_weight, innovation, scale_index):
    x = control[0]
    in_hbm = (x, obs_weight, innovation, scale_index)
    x_hbm, weight_hbm, innovation_hbm, classes = [pltpu.with_memory_space_constraint(v, pltpu.HBM) for v in in_hbm]
    member = members[0]
    levels, lat, columns = x.shape
    rows = levels * lat
    groups = lax.axis_size("member")
    share = levels // groups
    cells = float(groups * rows * columns * tiles)
    inverse = float(np.float32(1.0) / np.sqrt(np.float32(groups - 1)))
    half_pack = pltpu.VMEM((levels // 2, lat, columns), f32)
    field = pltpu.VMEM((levels, lat, columns), f32)
    part = pltpu.VMEM((share, lat, columns), f32)
    square = pltpu.VMEM((rows, rows), bf16)
    band = pltpu.VMEM((CLASSES * columns, 2 * columns), bf16)
    line = pltpu.VMEM((1, columns), f32)
    chips = [list(range(core, groups, 2)) for core in range(2)]
    cores = [[i, i + 1] for i in range(0, groups, 2)]
    near_pairs = [(i, i ^ 1) for i in range(tiles)]
    far_pairs = [(i, (((i - 1) % tiles ^ 1) + 1) % tiles) for i in range(tiles)]
    hbm = [pl.BlockSpec(memory_space=pltpu.HBM)]

    far, near, x_near = pl.pallas_call(
        pack_kernel,
        out_shape=(half_pack, half_pack, field),
        in_specs=hbm,
        out_specs=tuple(vmem(3)),
        scratch_shapes=[pltpu.SemaphoreType.DMA((PARTS, 2))],
        compiler_params=params(),
        name="pack_control",
    )(x_hbm)
    far = lax.ppermute(far, "tile", far_pairs)
    near = lax.ppermute(near, "tile", near_pairs)
    fh, fl, wide, mix, own, halo, hot, y, scaled, half_sum, weight_share, innovation_share = pl.pallas_call(
        functools.partial(operators_kernel, inverse),
        out_shape=(square, square, pltpu.VMEM((levels, rows), f32), pltpu.VMEM((lat, rows), f32), band, band, pltpu.VMEM((CLASSES, rows, columns), bf16), pltpu.VMEM((rows, columns), f32), field, line, part, part),
        in_specs=hbm + vmem(2) + hbm * 2,
        out_specs=tuple(vmem(12)),
        scratch_shapes=[
            pltpu.SMEM((levels,), jnp.int32),
            pltpu.VMEM((levels, columns), f32),
            pltpu.VMEM((rows, columns), f32),
            pltpu.SemaphoreType.DMA((3,)),
        ],
        compiler_params=params(),
        cost_estimate=pl.CostEstimate(flops=6 * rows * rows * columns, bytes_accessed=6 * 1024 * 1024, transcendentals=300000),
        name="operators",
    )(classes, x_near, member, weight_hbm, innovation_hbm)
    half_term = pltpu.VMEM((groups // 2, share, lat, columns), f32)
    mine, other = pl.pallas_call(
        forward_kernel,
        out_shape=(half_term, half_term),
        in_specs=vmem(8),
        out_specs=tuple(vmem(2)),
        compiler_params=params(),
        name="forward",
    )(far, near, y, fh, fl, halo, hot, scaled)
    sent = lax.all_gather(other, "member", axis_index_groups=cores)
    both = pl.pallas_call(add_kernel, out_shape=half_term, in_specs=vmem(2), out_specs=vmem(1)[0], compiler_params=params(), name="add_cores")(mine, sent)
    got = lax.all_to_all(both, "member", 0, 0, axis_index_groups=chips)
    inc, misfit_share, sums = pl.pallas_call(
        middle_kernel,
        out_shape=(part, pltpu.VMEM((groups // 2, share, lat, columns), f32), line),
        in_specs=vmem(4),
        out_specs=tuple(vmem(3)),
        compiler_params=params(),
        name="middle",
    )(got, weight_share, innovation_share, half_sum)
    misfit_mine = lax.all_to_all(misfit_share, "member", 0, 0, axis_index_groups=chips)
    misfit = lax.all_gather(misfit_mine, "member", axis_index_groups=cores)
    w, far, near = pl.pallas_call(
        weight_kernel,
        out_shape=(field, half_pack, half_pack),
        in_specs=vmem(2),
        out_specs=tuple(vmem(3)),
        compiler_params=params(),
        name="weighted",
    )(scaled, misfit)
    far = lax.ppermute(far, "tile", far_pairs)
    near = lax.ppermute(near, "tile", near_pairs)
    inner, ah, al = pl.pallas_call(
        local_kernel,
        out_shape=(field, square, square),
        in_specs=vmem(6),
        out_specs=tuple(vmem(3)),
        compiler_params=params(),
        cost_estimate=pl.CostEstimate(flops=8 * rows * rows * columns, bytes_accessed=4 * 1024 * 1024, transcendentals=0),
        name="local",
    )(w, x, own, hot, wide, mix)
    grad, sums = pl.pallas_call(
        adjoint_kernel,
        out_shape=(field, pltpu.VMEM((groups, 1, columns), f32)),
        in_specs=vmem(8),
        out_specs=tuple(vmem(2)),
        compiler_params=params(),
        name="adjoint",
    )(far, near, inner, halo, hot, ah, al, sums)
    sums = jnp.sum(lax.all_to_all(sums, "member", 0, 0), axis=0)
    sums = jnp.broadcast_to(sums[None], (tiles,) + sums.shape)
    one = pltpu.HBM((1, 1), f32)
    square_mean, cost, grad, inc = pl.pallas_call(
        functools.partial(finish_kernel, cells),
        out_shape=(one, one, pltpu.HBM(grad.shape, f32), pltpu.HBM(inc.shape, f32)),
        in_specs=vmem(3),
        out_specs=tuple(hbm * 4),
        scratch_shapes=[pltpu.VMEM((1, 1), f32), pltpu.VMEM((1, 1), f32), pltpu.SemaphoreType.DMA((4,))],
        compiler_params=params(),
        name="finish",
    )(lax.all_to_all(sums, "tile", 0, 0), grad, inc)
    return inc, grad[None], cost.reshape(()), square_mean.reshape(())


def solution(mesh):
    placed = (
        P("member", None, None, "tile"),
        P("member", None, None, "tile"),
        P(None, None, "tile"),
        P(None, None, "tile"),
        P(),
    )
    return jax.shard_map(
        functools.partial(per_device, mesh.shape["tile"]),
        mesh=mesh,
        in_specs=placed,
        out_specs=(P("member", None, "tile"), P("member", None, None, "tile"), P(), P()),
        check_vma=False,
    )
```
